128 devices in a mesh: stream: 8 (over y, core), azim: 16 (over z, x).
Axes of the slice: x: 4, y: 4, z: 4, core: 2. Of those that a mesh axis runs over, the one named last changes fastest.
Arguments:
- fluid: float32 [4, 512, 512, 128], P(None, 'stream', 'azim'), may hold values from -4 to 4
- bubbles: float32 [65536, 5, 128], P(('stream', 'azim'))
- counts: int32 [128], P(('stream', 'azim')), may hold values from 128 to 512
- outgoing_block_order: int32 [65536], P(('stream', 'azim')), may hold values from 0 to 511, as said below
- tiles_first_update: int32 [65536], P(('stream', 'azim')), may hold values from 0 to 2047
- tiles_after: int32 [65536], P(('stream', 'azim')), may hold values from 0 to 2047
Outputs:
- fluid_out: float32 [4, 512, 512, 128], P(None, 'stream', 'azim')
- bubbles_out: float32 [65536, 5, 128], P(('stream', 'azim'))
- void_fraction: float32 [512, 512, 128], P('stream', 'azim')
The draws below stay inside these ranges and needn't reach their ends.
Inputs may be any that keep to these rules, and one draw needn't show every extreme that they name: `outgoing_block_order`: for each device, its 512 entries are each of 0 to 511 once.
All inputs are finite; a program needn't handle non-finite values.
Results may differ from the reference program's by a relative error of at most 0.000076.
Values sent between devices are 32-bit elements; how exact they have to be, the bound alone decides.
No kernel may reach another device: no remote copies, remote signals or barrier semaphores. Data moves between devices by JAX's collectives and lax.ppermute only.
A program may use at most 128 MiB of HBM per device.

```python
import math
import jax
import jax.numpy as jnp
import numpy as np
from jax import lax

CS = 64
CA = 32
CR = 128
BB = 128
NBLK = 512
SUBSTEPS = 8
NTILE = 2048
CAP = 4
NS = 512
NAZ = 512
NBT = 65536
N_AZIM = 16
DEVICES = 128


def draw_bubbles(key, part):
    uniform_draw = jax.random.uniform(key, (NBT, 5, BB), jnp.float32)
    lower = jnp.array([0.8, -0.3, 4.0, -1.0, 0.8], jnp.float32)
    upper = jnp.array([1.25, 0.3, CR - 5.0, 1.0, 1.2], jnp.float32)
    return (lower[None, :, None] + (upper - lower)[None, :, None] * uniform_draw).astype(jnp.float32)


def draw_outgoing_block_order(key, part):
    device_keys = jax.random.split(jax.random.fold_in(key, 17), NBT // NBLK)
    orders = jax.vmap(lambda single: jax.random.permutation(single, NBLK))(device_keys)
    return orders.reshape(-1).astype(jnp.int32)


def plant(values, key, least, top_value):
    longest = values.shape.index(max(values.shape))
    spots = []
    for shift in (0, 1):
        where = [jax.random.randint(jax.random.fold_in(key, axis), (), 0, length) for axis, length in enumerate(values.shape)]
        where[longest] = (where[longest] + shift) % values.shape[longest]
        spots.append(tuple(where))
    return values.at[spots[0]].set(least).at[spots[1]].set(top_value)


def steps_of(key, shape, shards, low, largest):
    def one(dim, blocks):
        steps = jax.random.uniform(jax.random.fold_in(jax.random.fold_in(key, 6), dim), (blocks,), jnp.float32, low / len(shards), largest / len(shards))
        return jnp.repeat(jnp.exp(steps), shape[dim] // blocks).reshape((-1,) + (1,) * (len(shape) - dim - 1))

    loudness = one(*shards[0])
    for cut in shards[1:]:
        loudness = loudness * one(*cut)
    return loudness


def rank_bounds(amount, slope):
    weights = [(1 << 20) // math.isqrt(standing ** slope) + 1 for standing in range(1, amount + 1)]
    deviation = 1 + sum(weights) // (1 << 30)
    return np.cumsum(np.array([max(1, weight // deviation) for weight in weights]))


def skewed_ids(own_key, extent, amount, lean):
    table = rank_bounds(amount, lean)
    ticket = jax.random.randint(jax.random.fold_in(own_key, 1), extent, 0, int(table[amount - 1]))
    grade = jnp.searchsorted(jnp.asarray(table, jnp.int32), ticket, side="right")
    return jax.random.permutation(jax.random.fold_in(own_key, 2), amount)[grade].astype(jnp.int32)


def bell_draw(own_key, dims, deviation, bound, shards=(), kind=jnp.bfloat16):
    gain = steps_of(own_key, dims, shards, -0.22, 0.18) if shards else 1.0
    values = jax.random.normal(own_key, dims, jnp.float32) * deviation * gain
    return jnp.minimum(jnp.maximum(values, -bound), bound).astype(kind)


def setup_inputs(seed: int = 0) -> dict:
    key_of = jax.random.split(jax.random.key(seed), 7)
    fluid = bell_draw(key_of[0], (4, NS, NAZ, CR), 1.0, 4.0, ((1, 8), (2, 16)), jnp.float32)
    bubbles = draw_bubbles(jax.random.fold_in(key_of[6], 71), 0)
    counts = plant(jax.random.randint(key_of[2], (DEVICES,), NBLK // 4, NBLK + 1), jax.random.fold_in(key_of[2], 1), NBLK // 4, NBLK).astype(jnp.int32)
    outgoing_block_order = draw_outgoing_block_order(jax.random.fold_in(key_of[6], 71), 0)
    tiles_first_update = plant(skewed_ids(key_of[4], (NBT,), NTILE, 1), jax.random.fold_in(key_of[4], 3), 0, NTILE - 1).astype(jnp.int32)
    tiles_after = plant(skewed_ids(key_of[5], (NBT,), NTILE, 1), jax.random.fold_in(key_of[5], 3), 0, NTILE - 1).astype(jnp.int32)
    return {"fluid": fluid, "bubbles": bubbles, "counts": counts, "outgoing_block_order": outgoing_block_order, "tiles_first_update": tiles_first_update, "tiles_after": tiles_after}


TIME_STEP = 0.25
MEAN_FLOW = 0.5
DIFFUSION = 0.1
KERNEL_WIDTH = 1.5
GAS_INDEX = 4.2
PRESSURE_COUPLING = 0.3
AMBIENT = 1.0
RELAX_TIME = 0.5
VISCOUS = 0.08
SOURCE_GAIN = 0.05
VOID_SCALE = 0.01
FOUR_PI = 12.566370614359172


def kernel_weights(position, cell_centres):
    offset = (position[:, :, None] - cell_centres) / KERNEL_WIDTH
    raw = jnp.exp(-0.5 * offset * offset)
    return raw / jnp.sum(raw, axis=-1, keepdims=True)


def advance_group(packed_blocks):
    bubble_state, tile_row_count, alive_flags = packed_blocks
    cell_centres = jnp.arange(tile_row_count.shape[-1], dtype=jnp.int32).astype(jnp.float32)
    weights = kernel_weights(bubble_state[:, 2], cell_centres)
    sampled = jnp.einsum("gbk,gck->gcb", weights, tile_row_count, precision=lax.Precision.HIGHEST)
    pressure = sampled[:, 0]
    velocity = sampled[:, 1]
    radius = bubble_state[:, 0]
    growth = bubble_state[:, 1]
    position = bubble_state[:, 2]
    bubble_speed = bubble_state[:, 3]
    rest_radius = bubble_state[:, 4]
    substep_size = TIME_STEP / SUBSTEPS
    for substep in range(SUBSTEPS):
        gas = jnp.exp(GAS_INDEX * jnp.log(rest_radius / radius))
        accel = (gas - AMBIENT - PRESSURE_COUPLING * pressure - 1.5 * growth * growth - VISCOUS * growth / radius) / radius
        growth = growth + substep_size * accel
        radius = radius + substep_size * growth
        bubble_speed = bubble_speed + substep_size * (velocity - bubble_speed) / RELAX_TIME
        position = position + substep_size * bubble_speed
    new_state = jnp.stack([radius, growth, position, bubble_speed, rest_radius], axis=1)
    weights = kernel_weights(position, cell_centres)
    source_amounts = jnp.stack([SOURCE_GAIN * FOUR_PI * radius * radius * growth,
                         VOID_SCALE * FOUR_PI / 3.0 * radius * radius * radius], axis=1)
    source_amounts = source_amounts * alive_flags[:, None, None]
    spread_sources = jnp.einsum("gbk,gcb->gck", weights, source_amounts, precision=lax.Precision.HIGHEST)
    return new_state, spread_sources


def advance_every_group(bubble_state, tile_row_count, alive_flags):
    bubble_groups = bubble_state.shape[0] // 64
    new_state, spread_sources = lax.map(advance_group, (bubble_state.reshape((bubble_groups, 64) + bubble_state.shape[1:]),
                                                tile_row_count.reshape((bubble_groups, 64) + tile_row_count.shape[1:]),
                                                alive_flags.reshape(bubble_groups, 64)))
    return new_state.reshape(bubble_state.shape), spread_sources.reshape(tile_row_count.shape)


def fluid_update(flow_field, stream_up, stream_down, azim_up, azim_down, radial_up, radial_down, source):
    d_stream = 0.5 * (stream_up - stream_down)
    d_azim = 0.5 * (azim_up - azim_down)
    d_radial = 0.5 * (radial_up - radial_down)
    pressure_rate = -MEAN_FLOW * d_stream[0] - d_stream[1] - d_azim[2] - d_radial[3] - source
    stream_rate = -MEAN_FLOW * d_stream[1] - d_stream[0]
    azim_rate = -MEAN_FLOW * d_stream[2] - d_azim[0]
    radial_rate = -MEAN_FLOW * d_stream[3] - d_radial[0]
    change = jnp.stack([pressure_rate, stream_rate, azim_rate, radial_rate])
    laplace = stream_up + stream_down + azim_up + azim_down + radial_up + radial_down - 6.0 * flow_field
    return flow_field + TIME_STEP * change + DIFFUSION * laplace


def fluid_step(flow_field, source):
    padded = jnp.pad(flow_field, ((0, 0), (1, 1), (0, 0), (1, 1)))
    return fluid_update(flow_field, padded[:, 2:, :, 1:-1], padded[:, :-2, :, 1:-1],
                        jnp.roll(flow_field, -1, axis=2), jnp.roll(flow_field, 1, axis=2),
                        padded[:, 1:-1, :, 2:], padded[:, 1:-1, :, :-2], source)


def global_update(flow_field, bubble_state, tile_indices, alive_flags):
    slot_index = jnp.arange(NBT, dtype=jnp.int32)
    owner_device = slot_index // NBLK
    stream_cell = (owner_device // N_AZIM) * CS + tile_indices // CA
    azim_cell = (owner_device % N_AZIM) * CA + tile_indices % CA
    selected = jnp.stack([flow_field[0], flow_field[3]])
    tile_row_count = selected[:, stream_cell, azim_cell].transpose(1, 0, 2)
    bubble_state, spread_sources = advance_every_group(bubble_state, tile_row_count, alive_flags)
    grid = jnp.zeros((2,) + flow_field.shape[1:], jnp.float32).at[:, stream_cell, azim_cell].add(spread_sources.transpose(1, 0, 2))
    return fluid_step(flow_field, grid[0]), bubble_state, grid[1]


def reference(fluid, bubbles, counts, outgoing_block_order, tiles_first_update, tiles_after):
    slot_index = jnp.arange(NBT, dtype=jnp.int32)
    owner_device = slot_index // NBLK
    local_slot_index = slot_index % NBLK
    alive_flags = (local_slot_index < counts[owner_device]).astype(jnp.float32)
    flow_field, bubble_state, void_before_update = global_update(fluid, bubbles, tiles_first_update, alive_flags)
    source_device = local_slot_index // CAP
    within = local_slot_index % CAP
    position_sent = source_device * NBLK + owner_device * CAP + within
    sender_slot_index = (source_device * NBLK + outgoing_block_order[position_sent]).astype(jnp.int32)
    moved = bubble_state[sender_slot_index]
    moved_alive_flags = alive_flags[sender_slot_index]
    flow_field, bubble_state, void_field = global_update(flow_field, moved, tiles_after, moved_alive_flags)
    return flow_field, bubble_state * moved_alive_flags[:, None, None], void_field
```

```python
import functools

import jax
import jax.numpy as jnp
from jax import lax
from jax.experimental import pallas as pl
from jax.experimental.pallas import tpu as pltpu
from jax.sharding import PartitionSpec as P

SUBSTEPS = 8
TIME_STEP = 0.25
MEAN_FLOW = 0.5
DIFFUSION = 0.1
KERNEL_WIDTH = 1.5
GAS_INDEX = 4.2
PRESSURE_COUPLING = 0.3
AMBIENT = 1.0
RELAX_TIME = 0.5
VISCOUS = 0.08
SOURCE_GAIN = 0.05
VOID_SCALE = 0.01
FOUR_PI = 12.566370614359172
LOG2_E = 1.4426950408889634

CR = 128
BB = 128
NBLK = 512
COMPS = 5
CAP = 4
PACK = 24
GROUP = 8
CHUNK = 64
SHARP = 0.5 / (KERNEL_WIDTH * KERNEL_WIDTH) * LOG2_E
VMEM = pltpu.VMEM
SMEM = pltpu.SMEM


def split(values):
    high = values.astype(jnp.bfloat16)
    low = (values - high.astype(jnp.float32)).astype(jnp.bfloat16)
    return high, low


def centre_terms(position):
    centre = jnp.clip(jnp.floor(position + 0.5), 0.0, CR - 1.0)
    return centre * SHARP, 2.0 * position - centre


def raw_weights(cells, scaled_cells, near, far):
    return jnp.exp2((scaled_cells[...] - near) * (far - cells[...]))


def fill_cells(cells, scaled_cells):
    index = lax.broadcasted_iota(jnp.int32, (CR, BB), 0).astype(jnp.float32)
    cells[...] = index
    scaled_cells[...] = index * SHARP


def sample_phase(groups, state, rows_p, rows_v, cells, scaled_cells, sampled_p, sampled_v):
    sublane = lax.broadcasted_iota(jnp.int32, (GROUP, BB), 0)
    ones = jnp.ones((16, CR), jnp.bfloat16)

    def body(group, carry):
        base = pl.multiple_of(group * GROUP, GROUP)
        here = pl.ds(base, GROUP)
        near, far = centre_terms(state[here, 2, :])
        rows = jnp.concatenate([rows_p[here, :], rows_v[here, :]], axis=0)
        high, low = split(rows)
        left = jnp.concatenate([high, low, ones], axis=0)
        left = jnp.concatenate([left, left], axis=1)
        acc_p = jnp.zeros((GROUP, BB), jnp.float32)
        acc_v = acc_p
        acc_n = acc_p
        for i in range(GROUP):
            w = raw_weights(cells, scaled_cells, near[i : i + 1], far[i : i + 1])
            right = jnp.concatenate(split(w), axis=0)
            out = jnp.dot(left, right, preferred_element_type=jnp.float32)
            mine = sublane == i
            acc_p = jnp.where(mine, out[0:8] + out[16:24], acc_p)
            acc_v = jnp.where(mine, out[8:16] + out[24:32], acc_v)
            acc_n = jnp.where(mine, out[32:40], acc_n)
        sampled_p[here, :] = acc_p / acc_n
        sampled_v[here, :] = acc_v / acc_n
        return carry

    lax.fori_loop(0, groups, body, 0)


def bubble_phase(chunks, state, sampled_p, sampled_v, source, void):
    h = TIME_STEP / SUBSTEPS

    def body(chunk, carry):
        here = pl.ds(pl.multiple_of(chunk * CHUNK, CHUNK), CHUNK)
        radius = state[here, 0, :]
        growth = state[here, 1, :]
        position = state[here, 2, :]
        speed = state[here, 3, :]
        rest_log = jnp.log2(state[here, 4, :])
        drive = AMBIENT + PRESSURE_COUPLING * sampled_p[here, :]
        velocity = sampled_v[here, :]
        for _ in range(SUBSTEPS):
            inverse = 1.0 / radius
            gas = jnp.exp2(GAS_INDEX * (rest_log - jnp.log2(radius)))
            accel = (gas - drive - growth * (1.5 * growth + VISCOUS * inverse)) * inverse
            growth = growth + h * accel
            radius = radius + h * growth
            speed = speed + (h / RELAX_TIME) * (velocity - speed)
            position = position + h * speed
        state[here, 0, :] = radius
        state[here, 1, :] = growth
        state[here, 2, :] = position
        state[here, 3, :] = speed
        area = radius * radius
        source[here, :] = (SOURCE_GAIN * FOUR_PI) * area * growth
        if void is not None:
            void[here, :] = (VOID_SCALE * FOUR_PI / 3.0) * area * radius
        return carry

    lax.fori_loop(0, chunks, body, 0)


def spread_phase(groups, live_blocks, tile_of, state, amounts, cells, scaled_cells, grids):
    sublane = lax.broadcasted_iota(jnp.int32, (GROUP, BB), 0)
    kinds = len(amounts)

    def body(group, carry):
        base = pl.multiple_of(group * GROUP, GROUP)
        here = pl.ds(base, GROUP)
        near, far = centre_terms(state[here, 2, :])
        whole = jnp.concatenate([a[here, :] for a in amounts], axis=0)
        accs = [jnp.zeros((GROUP, CR), jnp.float32) for _ in amounts]
        for i in range(GROUP):
            w = raw_weights(cells, scaled_cells, near[i : i + 1], far[i : i + 1])
            total = jnp.sum(w, axis=0, keepdims=True)
            high, low = split(w)
            right = jnp.concatenate([high, low], axis=1)
            top, rest = split(whole * (1.0 / total))
            left = jnp.concatenate([top, rest], axis=0)
            left = jnp.concatenate([left, left], axis=1)
            out = lax.dot_general(
                left, right, (((1,), (1,)), ((), ())), preferred_element_type=jnp.float32
            )
            mine = sublane == i
            for kind in range(kinds):
                lo = GROUP * kind
                hi = GROUP * (kinds + kind)
                accs[kind] = jnp.where(mine, out[lo : lo + GROUP] + out[hi : hi + GROUP], accs[kind])
        alive = sublane + base < live_blocks
        accs = [jnp.where(alive, acc, 0.0) for acc in accs]
        for i in range(GROUP):
            tile = tile_of(base + i)
            for grid, acc in zip(grids, accs):
                grid[pl.ds(tile, 1), :] = grid[pl.ds(tile, 1), :] + acc[i : i + 1]
        return carry

    lax.fori_loop(0, groups, body, 0)


def first_bubbles_kernel(
    counts, order, tiles, bubbles, flow_p, flow_v, packed, source_grid,
    state, rows_p, rows_v, sampled_p, sampled_v, source, cells, scaled_cells,
):
    live = counts[0]
    groups = (live + GROUP - 1) // GROUP
    chunks = (live + CHUNK - 1) // CHUNK
    fill_cells(cells, scaled_cells)
    source_grid[...] = jnp.zeros_like(source_grid)

    def gather(group, carry):
        base = pl.multiple_of(group * GROUP, GROUP)
        for i in range(GROUP):
            tile = tiles[base + i]
            rows_p[pl.ds(base + i, 1), :] = flow_p[0, pl.ds(tile, 1), :]
            rows_v[pl.ds(base + i, 1), :] = flow_v[0, pl.ds(tile, 1), :]
            state[base + i, 0:COMPS, :] = bubbles[base + i]
        return carry

    lax.fori_loop(0, groups, gather, 0)
    sample_phase(groups, state, rows_p, rows_v, cells, scaled_cells, sampled_p, sampled_v)
    bubble_phase(chunks, state, sampled_p, sampled_v, source, None)
    spread_phase(
        groups, live, lambda j: tiles[j], state, [source], cells, scaled_cells, [source_grid]
    )

    def pack(peer, carry):
        for k in range(CAP):
            block = order[peer * CAP + k]
            alive = block < live
            packed[peer, COMPS * k : COMPS * (k + 1), :] = jnp.where(
                alive, state[block, 0:COMPS, :], 0.0
            )
            packed[peer, COMPS * CAP + k : COMPS * CAP + k + 1, :] = jnp.where(
                alive, jnp.ones((1, BB), jnp.float32), 0.0
            )
        return carry

    lax.fori_loop(0, NBLK // CAP, pack, 0)


def second_bubbles_kernel(
    alive, tiles, packed, flow_p, flow_v, bubbles_out, source_grid, void_grid,
    slots, arrived, state, rows_p, rows_v, sampled_p, sampled_v, source, void, cells, scaled_cells,
):
    fill_cells(cells, scaled_cells)
    source_grid[...] = jnp.zeros_like(source_grid)
    void_grid[...] = jnp.zeros_like(void_grid)
    bubbles_out[...] = jnp.zeros_like(bubbles_out)

    def unpack(peer, live):
        for k in range(CAP):
            slot = peer * CAP + k
            arrived[slot, 0:COMPS, :] = packed[peer, COMPS * k : COMPS * (k + 1), :]
            slots[live] = slot
            live = live + alive[slot]
        return live

    live = lax.fori_loop(0, NBLK // CAP, unpack, jnp.int32(0))
    last = slots[jnp.maximum(live - 1, 0)]
    for i in range(GROUP):
        slots[live + i] = last
    groups = (live + GROUP - 1) // GROUP
    chunks = (live + CHUNK - 1) // CHUNK

    def gather(group, carry):
        base = pl.multiple_of(group * GROUP, GROUP)
        for i in range(GROUP):
            slot = slots[base + i]
            tile = tiles[slot]
            rows_p[pl.ds(base + i, 1), :] = flow_p[0, pl.ds(tile, 1), :]
            rows_v[pl.ds(base + i, 1), :] = flow_v[0, pl.ds(tile, 1), :]
            state[base + i, 0:COMPS, :] = arrived[slot, 0:COMPS, :]
        return carry

    lax.fori_loop(0, groups, gather, 0)
    sample_phase(groups, state, rows_p, rows_v, cells, scaled_cells, sampled_p, sampled_v)
    bubble_phase(chunks, state, sampled_p, sampled_v, source, void)

    def put(group, carry):
        base = pl.multiple_of(group * GROUP, GROUP)
        for i in range(GROUP):
            bubbles_out[slots[base + i]] = state[base + i, 0:COMPS, :]
        return carry

    lax.fori_loop(0, groups, put, 0)
    spread_phase(
        groups, live, lambda j: tiles[slots[j]], state, [source, void], cells, scaled_cells,
        [source_grid, void_grid],
    )


def fluid_kernel(
    flow, source, stream_before, stream_after, azim_before, azim_after, new, *faces
):
    streams = flow.shape[1]
    azims = flow.shape[2]
    shape = (azims, CR)
    lane = lax.broadcasted_iota(jnp.int32, shape, 1)
    row = lax.broadcasted_iota(jnp.int32, shape, 0)
    first_lane, last_lane = lane == 0, lane == CR - 1
    first_row, last_row = row == 0, row == azims - 1
    a = 0.5 * TIME_STEP

    def plane(s, down, up):
        sums = []
        values = []
        advected = []
        stream_slope = []
        azim_slope = {}
        radial_slope = {}
        for c in range(4):
            f = flow[c, s]
            before = down(c)
            after = up(c)
            left = jnp.where(first_row, azim_before[c, pl.ds(s, 1), :], pltpu.roll(f, 1, 0))
            right = jnp.where(last_row, azim_after[c, pl.ds(s, 1), :], pltpu.roll(f, azims - 1, 0))
            inner = jnp.where(first_lane, 0.0, pltpu.roll(f, 1, 1))
            outer = jnp.where(last_lane, 0.0, pltpu.roll(f, CR - 1, 1))
            slope = after - before
            values.append(f)
            sums.append(((before + after) + (left + right)) + (inner + outer))
            stream_slope.append(slope)
            if c in (0, 2):
                azim_slope[c] = right - left
            if c in (0, 3):
                radial_slope[c] = outer - inner
        rates = [
            MEAN_FLOW * stream_slope[0] + stream_slope[1] + azim_slope[2] + radial_slope[3],
            MEAN_FLOW * stream_slope[1] + stream_slope[0],
            MEAN_FLOW * stream_slope[2] + azim_slope[0],
            MEAN_FLOW * stream_slope[3] + radial_slope[0],
        ]
        for c in range(4):
            value = (1.0 - 6.0 * DIFFUSION) * values[c] + DIFFUSION * sums[c] - a * rates[c]
            if c == 0:
                value = value - TIME_STEP * source[s]
            new[c, s] = value
            if faces:
                faces[2][c, pl.ds(s, 1), :] = value[0:1]
                faces[3][c, pl.ds(s, 1), :] = value[azims - 1 : azims]

    plane(0, lambda c: stream_before[c], lambda c: flow[c, 1])

    def body(s, carry):
        plane(s, lambda c: flow[c, s - 1], lambda c: flow[c, s + 1])
        return carry

    lax.fori_loop(1, streams - 1, body, 0)
    plane(streams - 1, lambda c: flow[c, streams - 2], lambda c: stream_after[c])
    if faces:
        faces[0][...] = new[:, 0]
        faces[1][...] = new[:, streams - 1]


F32 = jnp.float32
SHAPE = jax.ShapeDtypeStruct


def whole(shape):
    return pl.BlockSpec(shape, lambda *_: (0,) * len(shape), memory_space=VMEM)


def component(c, tiles):
    return pl.BlockSpec((1, tiles, CR), lambda *_: (c, 0, 0), memory_space=VMEM)


def params(mib):
    return pltpu.CompilerParams(vmem_limit_bytes=mib << 20)


def bubble_scratch(amounts):
    wide = [VMEM((NBLK, BB), F32)] * (4 + amounts)
    return [VMEM((NBLK, 8, BB), F32)] + wide + [VMEM((CR, BB), F32)] * 2


def first_bubbles(counts, order, tiles, bubbles, flow_rows):
    ntile = flow_rows.shape[1]
    peers = NBLK // CAP
    return pl.pallas_call(
        first_bubbles_kernel,
        grid=(1,),
        in_specs=[pl.BlockSpec(memory_space=SMEM)] * 3
        + [whole((NBLK, COMPS, BB)), component(0, ntile), component(3, ntile)],
        out_specs=[whole((peers, PACK, BB)), whole((ntile, CR))],
        out_shape=[SHAPE((peers, PACK, BB), F32), SHAPE((ntile, CR), F32)],
        scratch_shapes=bubble_scratch(1),
        compiler_params=params(24),
        cost_estimate=pl.CostEstimate(flops=10**9, bytes_accessed=40 * 10**6, transcendentals=10**7),
        name="first_bubbles",
    )(counts, order, tiles, bubbles, flow_rows, flow_rows)


def second_bubbles(alive, tiles, packed, flow_rows):
    ntile = flow_rows.shape[1]
    peers = NBLK // CAP
    return pl.pallas_call(
        second_bubbles_kernel,
        grid=(1,),
        in_specs=[pl.BlockSpec(memory_space=SMEM)] * 2
        + [whole((peers, PACK, BB)), component(0, ntile), component(3, ntile)],
        out_specs=[whole((NBLK, COMPS, BB)), whole((ntile, CR)), whole((ntile, CR))],
        out_shape=[SHAPE((NBLK, COMPS, BB), F32), SHAPE((ntile, CR), F32), SHAPE((ntile, CR), F32)],
        scratch_shapes=[SMEM((NBLK + 2 * GROUP,), jnp.int32), VMEM((NBLK, 8, BB), F32)]
        + bubble_scratch(2),
        compiler_params=params(24),
        cost_estimate=pl.CostEstimate(flops=10**9, bytes_accessed=40 * 10**6, transcendentals=10**7),
        name="second_bubbles",
    )(alive, tiles, packed, flow_rows, flow_rows)


def fluid_update(flow, source, halos, with_faces):
    streams, azims = flow.shape[1:3]
    out_shape = [SHAPE(flow.shape, F32)]
    if with_faces:
        out_shape += [SHAPE((4, azims, CR), F32)] * 2 + [SHAPE((4, streams, CR), F32)] * 2
    return pl.pallas_call(
        fluid_kernel,
        grid=(1,),
        in_specs=[whole(flow.shape), whole((streams, azims, CR))]
        + [whole((4, azims, CR))] * 2
        + [whole((4, streams, CR))] * 2,
        out_specs=[whole(s.shape) for s in out_shape],
        out_shape=out_shape,
        compiler_params=params(28),
        cost_estimate=pl.CostEstimate(flops=10**8, bytes_accessed=10**7, transcendentals=0),
        name="fluid",
    )(flow, source.reshape(streams, azims, CR), *halos)


def exchange(head_stream, tail_stream, head_azim, tail_azim):
    streams = lax.axis_size("stream")
    azims = lax.axis_size("azim")
    return (
        lax.ppermute(tail_stream, "stream", [(i, i + 1) for i in range(streams - 1)]),
        lax.ppermute(head_stream, "stream", [(i + 1, i) for i in range(streams - 1)]),
        lax.ppermute(tail_azim, "azim", [(i, (i + 1) % azims) for i in range(azims)]),
        lax.ppermute(head_azim, "azim", [((i + 1) % azims, i) for i in range(azims)]),
    )


def on_device(fluid, bubbles, counts, outgoing_block_order, tiles_first_update, tiles_after):
    halos = exchange(fluid[:, 0], fluid[:, -1], fluid[:, :, 0], fluid[:, :, -1])
    rows = fluid.reshape(4, -1, CR)
    packed, source = first_bubbles(
        counts, outgoing_block_order, tiles_first_update, bubbles, rows
    )
    arrived = lax.all_to_all(packed, ("stream", "azim"), split_axis=0, concat_axis=0, tiled=True)
    flow, *faces = fluid_update(fluid, source, halos, True)
    halos = exchange(*faces)
    alive = (arrived[:, COMPS * CAP :, 0] > 0.5).astype(jnp.int32).reshape(-1)
    moved, source, void = second_bubbles(alive, tiles_after, arrived, flow.reshape(4, -1, CR))
    (flow,) = fluid_update(flow, source, halos, False)
    return flow, moved, void.reshape(fluid.shape[1:])


def solution(mesh):
    return jax.shard_map(
        on_device,
        mesh=mesh,
        in_specs=(
            P(None, "stream", "azim", None),
            P(("stream", "azim"), None, None),
            P(("stream", "azim")),
            P(("stream", "azim")),
            P(("stream", "azim")),
            P(("stream", "azim")),
        ),
        out_specs=(
            P(None, "stream", "azim", None),
            P(("stream", "azim"), None, None),
            P("stream", "azim", None),
        ),
        check_vma=False,
    )
```

```python
import functools

import jax
import jax.numpy as jnp
from jax import lax
from jax.experimental import pallas as pl
from jax.experimental.pallas import tpu as pltpu
from jax.sharding import PartitionSpec as P

SUBSTEPS = 8
TIME_STEP = 0.25
MEAN_FLOW = 0.5
DIFFUSION = 0.1
KERNEL_WIDTH = 1.5
GAS_INDEX = 4.2
PRESSURE_COUPLING = 0.3
AMBIENT = 1.0
RELAX_TIME = 0.5
VISCOUS = 0.08
SOURCE_GAIN = 0.05
VOID_SCALE = 0.01
FOUR_PI = 12.566370614359172
LOG2_E = 1.4426950408889634

CR = 128
BB = 128
NBLK = 512
COMPS = 5
CAP = 4
PACK = 24
GROUP = 8
STREAM_BLOCK = 8
VMEM_MIB = 58
CHUNK = 64
SHARP = 0.5 / (KERNEL_WIDTH * KERNEL_WIDTH) * LOG2_E
VMEM = pltpu.VMEM
SMEM = pltpu.SMEM


def split(values):
    high = values.astype(jnp.bfloat16)
    low = (values - high.astype(jnp.float32)).astype(jnp.bfloat16)
    return high, low


def centre_terms(position):
    centre = jnp.clip(jnp.floor(position + 0.5), 0.0, CR - 1.0)
    return centre * SHARP, 2.0 * position - centre


def raw_weights(cells, scaled_cells, near, far):
    return jnp.exp2((scaled_cells[...] - near) * (far - cells[...]))


def fill_cells(cells, scaled_cells):
    index = lax.broadcasted_iota(jnp.int32, (CR, BB), 0).astype(jnp.float32)
    cells[...] = index
    scaled_cells[...] = index * SHARP


def sample_phase(groups, positions, rows_p, rows_v, cells, scaled_cells, sampled_p, sampled_v):
    sublane = lax.broadcasted_iota(jnp.int32, (GROUP, BB), 0)
    ones = jnp.ones((16, CR), jnp.bfloat16)

    def body(group, carry):
        base = pl.multiple_of(group * GROUP, GROUP)
        here = pl.ds(base, GROUP)
        near, far = centre_terms(positions(here))
        rows = jnp.concatenate([rows_p[here, :], rows_v[here, :]], axis=0)
        high, low = split(rows)
        left = jnp.concatenate([high, low, ones], axis=0)
        left = jnp.concatenate([left, left], axis=1)
        acc_p = jnp.zeros((GROUP, BB), jnp.float32)
        acc_v = acc_p
        acc_n = acc_p
        for i in range(0, GROUP, 2):
            right = jnp.concatenate(
                [
                    jnp.concatenate(
                        split(raw_weights(cells, scaled_cells, near[b : b + 1], far[b : b + 1])), axis=0
                    )
                    for b in (i, i + 1)
                ],
                axis=1,
            )
            both = jnp.dot(left, right, preferred_element_type=jnp.float32)
            for b, out in ((i, both[:, :BB]), (i + 1, both[:, BB:])):
                mine = sublane == b
                acc_p = jnp.where(mine, out[0:8] + out[16:24], acc_p)
                acc_v = jnp.where(mine, out[8:16] + out[24:32], acc_v)
                acc_n = jnp.where(mine, out[32:40], acc_n)
        sampled_p[here, :] = acc_p / acc_n
        sampled_v[here, :] = acc_v / acc_n
        return carry

    lax.fori_loop(0, groups, body, 0)


def bubble_phase(chunks, component, state, sampled_p, sampled_v, source, void):
    h = TIME_STEP / SUBSTEPS

    def body(chunk, carry):
        here = pl.ds(pl.multiple_of(chunk * CHUNK, CHUNK), CHUNK)
        radius = component(0, here)
        growth = component(1, here)
        position = component(2, here)
        speed = component(3, here)
        rest_log = jnp.log2(component(4, here))
        drive = AMBIENT + PRESSURE_COUPLING * sampled_p[here, :]
        velocity = sampled_v[here, :]
        for _ in range(SUBSTEPS):
            inverse = 1.0 / radius
            gas = jnp.exp2(GAS_INDEX * (rest_log - jnp.log2(radius)))
            accel = (gas - drive - growth * (1.5 * growth + VISCOUS * inverse)) * inverse
            growth = growth + h * accel
            radius = radius + h * growth
            speed = speed + (h / RELAX_TIME) * (velocity - speed)
            position = position + h * speed
        state[here, 0, :] = radius
        state[here, 1, :] = growth
        state[here, 2, :] = position
        state[here, 3, :] = speed
        state[here, 4, :] = component(4, here)
        area = radius * radius
        source[here, :] = (SOURCE_GAIN * FOUR_PI) * area * growth
        if void is not None:
            void[here, :] = (VOID_SCALE * FOUR_PI / 3.0) * area * radius
        return carry

    lax.fori_loop(0, chunks, body, 0)


def spread_phase(groups, live_blocks, tile_of, state, amounts, cells, scaled_cells, grids):
    sublane = lax.broadcasted_iota(jnp.int32, (GROUP, BB), 0)
    kinds = len(amounts)

    def body(group, carry):
        base = pl.multiple_of(group * GROUP, GROUP)
        here = pl.ds(base, GROUP)
        near, far = centre_terms(state[here, 2, :])
        whole = jnp.concatenate([a[here, :] for a in amounts], axis=0)
        accs = [jnp.zeros((GROUP, CR), jnp.float32) for _ in amounts]
        for i in range(0, GROUP, 2):
            lefts = []
            rights = []
            for b in (i, i + 1):
                w = raw_weights(cells, scaled_cells, near[b : b + 1], far[b : b + 1])
                total = jnp.sum(w, axis=0, keepdims=True)
                rights.append(jnp.concatenate(split(w), axis=1))
                left = jnp.concatenate(split(whole * (1.0 / total)), axis=0)
                lefts.append(jnp.concatenate([left, left], axis=1))
            left = jnp.concatenate(lefts, axis=0)
            right = jnp.concatenate(rights, axis=0)
            both = lax.dot_general(
                left, right, (((1,), (1,)), ((), ())), preferred_element_type=jnp.float32
            )
            for b in (0, 1):
                out = both[2 * GROUP * kinds * b :, CR * b : CR * (b + 1)]
                mine = sublane == i + b
                for kind in range(kinds):
                    lo = GROUP * kind
                    hi = GROUP * (kinds + kind)
                    accs[kind] = jnp.where(
                        mine, out[lo : lo + GROUP] + out[hi : hi + GROUP], accs[kind]
                    )
        alive = sublane + base < live_blocks
        accs = [jnp.where(alive, acc, 0.0) for acc in accs]
        for i in range(GROUP):
            tile = tile_of(base + i)
            for grid, acc in zip(grids, accs):
                grid[pl.ds(tile, 1), :] = grid[pl.ds(tile, 1), :] + acc[i : i + 1]
        return carry

    lax.fori_loop(0, groups, body, 0)


def first_bubbles_kernel(
    counts, order, tiles, bubbles, flow_p, flow_v, packed, source_grid,
    state, rows_p, rows_v, sampled_p, sampled_v, source, cells, scaled_cells,
):
    live = counts[0]
    groups = (live + GROUP - 1) // GROUP
    chunks = (live + CHUNK - 1) // CHUNK
    fill_cells(cells, scaled_cells)
    source_grid[...] = jnp.zeros_like(source_grid)

    def gather(group, carry):
        base = pl.multiple_of(group * GROUP, GROUP)
        for i in range(GROUP):
            tile = tiles[base + i]
            rows_p[pl.ds(base + i, 1), :] = flow_p[0, pl.ds(tile, 1), :]
            rows_v[pl.ds(base + i, 1), :] = flow_v[0, pl.ds(tile, 1), :]
        return carry

    lax.fori_loop(0, groups, gather, 0)
    sample_phase(
        groups, lambda here: bubbles[2, here, :], rows_p, rows_v, cells, scaled_cells, sampled_p, sampled_v
    )
    bubble_phase(
        chunks, lambda c, here: bubbles[c, here, :], state, sampled_p, sampled_v, source, None
    )
    spread_phase(
        groups, live, lambda j: tiles[j], state, [source], cells, scaled_cells, [source_grid]
    )

    lane = lax.broadcasted_iota(jnp.int32, (PACK - COMPS * CAP, BB), 1)

    def pack(peer, carry):
        flags = jnp.zeros((PACK - COMPS * CAP, BB), jnp.float32)
        for k in range(CAP):
            block = order[peer * CAP + k]
            alive = block < live
            packed[peer, COMPS * k : COMPS * (k + 1), :] = jnp.where(
                alive, state[block, 0:COMPS, :], 0.0
            )
            flags = jnp.where((lane == k) & alive, 1.0, flags)
        packed[peer, COMPS * CAP : PACK, :] = flags
        return carry

    lax.fori_loop(0, NBLK // CAP, pack, 0)


def second_bubbles_kernel(
    tiles, packed, flow_p, flow_v, bubbles_out, source_grid, void_grid,
    slots, flags, flag_sem, arrived, state, rows_p, rows_v, sampled_p, sampled_v, source, void, cells, scaled_cells,
):
    copy = pltpu.make_async_copy(packed.at[:, COMPS * CAP, :], flags, flag_sem)
    copy.start()
    fill_cells(cells, scaled_cells)
    source_grid[...] = jnp.zeros_like(source_grid)
    void_grid[...] = jnp.zeros_like(void_grid)

    def unpack(peer, carry):
        for k in range(CAP):
            arrived[peer * CAP + k, 0:COMPS, :] = packed[peer, COMPS * k : COMPS * (k + 1), :]
        return carry

    lax.fori_loop(0, NBLK // CAP, unpack, 0, unroll=4)
    copy.wait()

    def compact(peer, live):
        for k in range(CAP):
            slots[live] = peer * CAP + k
            live = live + jnp.where(flags[peer, k] > 0.5, 1, 0)
        return live

    live = lax.fori_loop(0, NBLK // CAP, compact, jnp.int32(0), unroll=4)
    last = slots[jnp.maximum(live - 1, 0)]
    for i in range(GROUP):
        slots[live + i] = last
    groups = (live + GROUP - 1) // GROUP
    chunks = (live + CHUNK - 1) // CHUNK

    def gather(group, carry):
        base = pl.multiple_of(group * GROUP, GROUP)
        for i in range(GROUP):
            slot = slots[base + i]
            tile = tiles[slot]
            rows_p[pl.ds(base + i, 1), :] = flow_p[0, pl.ds(tile, 1), :]
            rows_v[pl.ds(base + i, 1), :] = flow_v[0, pl.ds(tile, 1), :]
            state[base + i, 0:COMPS, :] = arrived[slot, 0:COMPS, :]
        return carry

    lax.fori_loop(0, groups, gather, 0)
    sample_phase(
        groups, lambda here: state[here, 2, :], rows_p, rows_v, cells, scaled_cells, sampled_p, sampled_v
    )
    bubble_phase(
        chunks, lambda c, here: state[here, c, :], state, sampled_p, sampled_v, source, void
    )
    arrived[...] = jnp.zeros_like(arrived)

    def put(group, carry):
        base = pl.multiple_of(group * GROUP, GROUP)
        for i in range(GROUP):
            arrived[slots[base + i]] = state[base + i]
        return carry

    lax.fori_loop(0, groups, put, 0)

    def store(group, carry):
        here = pl.ds(pl.multiple_of(group * GROUP, GROUP), GROUP)
        for c in range(COMPS):
            bubbles_out[c, here, :] = arrived[here, c, :]
        return carry

    lax.fori_loop(0, NBLK // GROUP, store, 0)
    spread_phase(
        groups, live, lambda j: tiles[slots[j]], state, [source, void], cells, scaled_cells,
        [source_grid, void_grid],
    )


def fluid_kernel(
    flow, flow_before, flow_after, source, stream_before, stream_after, azim_before, azim_after, new, *faces
):
    step = pl.program_id(0)
    first, final = step == 0, step == pl.num_programs(0) - 1
    streams = flow.shape[1]
    azims = flow.shape[2]
    shape = (azims, CR)
    lane = lax.broadcasted_iota(jnp.int32, shape, 1)
    row = lax.broadcasted_iota(jnp.int32, shape, 0)
    first_lane, last_lane = lane == 0, lane == CR - 1
    first_row, last_row = row == 0, row == azims - 1
    a = 0.5 * TIME_STEP

    def plane(s, down, up):
        sums = []
        values = []
        stream_slope = []
        azim_slope = {}
        radial_slope = {}
        for c in range(4):
            f = flow[c, s]
            before = down(c)
            after = up(c)
            left = jnp.where(first_row, azim_before[c, pl.ds(s, 1), :], pltpu.roll(f, 1, 0))
            right = jnp.where(last_row, azim_after[c, pl.ds(s, 1), :], pltpu.roll(f, azims - 1, 0))
            inner = jnp.where(first_lane, 0.0, pltpu.roll(f, 1, 1))
            outer = jnp.where(last_lane, 0.0, pltpu.roll(f, CR - 1, 1))
            values.append(f)
            sums.append(((before + after) + (left + right)) + (inner + outer))
            stream_slope.append(after - before)
            if c in (0, 2):
                azim_slope[c] = right - left
            if c in (0, 3):
                radial_slope[c] = outer - inner
        rates = [
            MEAN_FLOW * stream_slope[0] + stream_slope[1] + azim_slope[2] + radial_slope[3],
            MEAN_FLOW * stream_slope[1] + stream_slope[0],
            MEAN_FLOW * stream_slope[2] + azim_slope[0],
            MEAN_FLOW * stream_slope[3] + radial_slope[0],
        ]
        for c in range(4):
            value = (1.0 - 6.0 * DIFFUSION) * values[c] + DIFFUSION * sums[c] - a * rates[c]
            if c == 0:
                value = value - TIME_STEP * source[s]
            new[c, s] = value
            if faces:
                faces[2][c, pl.ds(s, 1), :] = value[0:1]
                faces[3][c, pl.ds(s, 1), :] = value[azims - 1 : azims]

    for s in range(streams):
        plane(
            s,
            (lambda c: jnp.where(first, stream_before[c], flow_before[c, 0])) if s == 0 else (lambda c: flow[c, s - 1]),
            (lambda c: jnp.where(final, stream_after[c], flow_after[c, 0])) if s == streams - 1 else (lambda c: flow[c, s + 1]),
        )
    if faces:

        @pl.when(first)
        def _():
            faces[0][...] = new[:, 0]

        @pl.when(final)
        def _():
            faces[1][...] = new[:, streams - 1]


F32 = jnp.float32
SHAPE = jax.ShapeDtypeStruct


def whole(shape):
    return pl.BlockSpec(shape, lambda *_: (0,) * len(shape), memory_space=VMEM)


def component(c, tiles):
    return pl.BlockSpec((1, tiles, CR), lambda *_: (c, 0, 0), memory_space=VMEM)


def params():
    return pltpu.CompilerParams(vmem_limit_bytes=VMEM_MIB << 20)


def bubble_scratch(amounts):
    wide = [VMEM((NBLK, BB), F32)] * (4 + amounts)
    return [VMEM((NBLK, 8, BB), F32)] + wide + [VMEM((CR, BB), F32)] * 2


def first_bubbles(counts, order, tiles, bubbles, flow_rows):
    ntile = flow_rows.shape[1]
    peers = NBLK // CAP
    return pl.pallas_call(
        first_bubbles_kernel,
        grid=(1,),
        in_specs=[pl.BlockSpec(memory_space=SMEM)] * 3
        + [whole((COMPS, NBLK, BB)), component(0, ntile), component(3, ntile)],
        out_specs=[whole((peers, PACK, BB)), whole((ntile, CR))],
        out_shape=[SHAPE((peers, PACK, BB), F32), SHAPE((ntile, CR), F32)],
        scratch_shapes=bubble_scratch(1),
        compiler_params=params(),
        cost_estimate=pl.CostEstimate(flops=10**9, bytes_accessed=10**8, transcendentals=10**7),
        name="first_bubbles",
    )(counts, order, tiles, bubbles, flow_rows, flow_rows)


def second_bubbles(tiles, packed, flow_rows):
    ntile = flow_rows.shape[1]
    peers = NBLK // CAP
    return pl.pallas_call(
        second_bubbles_kernel,
        grid=(1,),
        in_specs=[pl.BlockSpec(memory_space=SMEM)]
        + [whole((peers, PACK, BB)), component(0, ntile), component(3, ntile)],
        out_specs=[whole((COMPS, NBLK, BB)), whole((ntile, CR)), whole((ntile, CR))],
        out_shape=[SHAPE((COMPS, NBLK, BB), F32), SHAPE((ntile, CR), F32), SHAPE((ntile, CR), F32)],
        scratch_shapes=[
            SMEM((NBLK + 2 * GROUP,), jnp.int32),
            SMEM((peers, BB), F32),
            pltpu.SemaphoreType.DMA,
            VMEM((NBLK, 8, BB), F32),
        ]
        + bubble_scratch(2),
        compiler_params=params(),
        cost_estimate=pl.CostEstimate(flops=10**9, bytes_accessed=10**8, transcendentals=10**7),
        name="second_bubbles",
    )(tiles, packed, flow_rows, flow_rows)


def fluid_update(flow, source, halos, with_faces):
    streams, azims = flow.shape[1:3]
    out_shape = [SHAPE(flow.shape, F32)]
    if with_faces:
        out_shape += [SHAPE((4, azims, CR), F32)] * 2 + [SHAPE((4, streams, CR), F32)] * 2
    slab = STREAM_BLOCK
    moving = pl.BlockSpec((4, slab, azims, CR), lambda i: (0, i, 0, 0))
    along = pl.BlockSpec((4, slab, CR), lambda i: (0, i, 0))
    fixed = pl.BlockSpec((4, azims, CR), lambda i: (0, 0, 0))
    return pl.pallas_call(
        fluid_kernel,
        grid=(streams // slab,),
        in_specs=[
            moving,
            pl.BlockSpec((4, 1, azims, CR), lambda i: (0, jnp.maximum(i * slab - 1, 0), 0, 0)),
            pl.BlockSpec((4, 1, azims, CR), lambda i: (0, jnp.minimum((i + 1) * slab, streams - 1), 0, 0)),
            pl.BlockSpec((slab, azims, CR), lambda i: (i, 0, 0)),
            fixed,
            fixed,
            along,
            along,
        ],
        out_specs=[moving, fixed, fixed, along, along] if with_faces else [moving],
        out_shape=out_shape,
        compiler_params=params(),
        cost_estimate=pl.CostEstimate(flops=10**8, bytes_accessed=3 * 10**7, transcendentals=0),
        name="fluid",
    )(flow, flow, flow, source.reshape(streams, azims, CR), *halos)


def exchange(head_stream, tail_stream, head_azim, tail_azim):
    streams = lax.axis_size("stream")
    azims = lax.axis_size("azim")
    return (
        lax.ppermute(tail_stream, "stream", [(i, i + 1) for i in range(streams - 1)]),
        lax.ppermute(head_stream, "stream", [(i + 1, i) for i in range(streams - 1)]),
        lax.ppermute(tail_azim, "azim", [(i, (i + 1) % azims) for i in range(azims)]),
        lax.ppermute(head_azim, "azim", [((i + 1) % azims, i) for i in range(azims)]),
    )


def on_device(fluid, bubbles, counts, outgoing_block_order, tiles_first_update, tiles_after):
    halos = exchange(fluid[:, 0], fluid[:, -1], fluid[:, :, 0], fluid[:, :, -1])
    rows = fluid.reshape(4, -1, CR)
    packed, source = first_bubbles(
        counts, outgoing_block_order, tiles_first_update, bubbles.transpose(1, 0, 2), rows
    )
    packed, halos = lax.optimization_barrier((packed, halos))
    arrived = lax.all_to_all(packed, ("stream", "azim"), split_axis=0, concat_axis=0, tiled=True)
    flow, *faces = fluid_update(fluid, source, halos, True)
    halos = exchange(*faces)
    moved, source, void = second_bubbles(tiles_after, arrived, flow.reshape(4, -1, CR))
    (flow,) = fluid_update(flow, source, halos, False)
    return flow, moved.transpose(1, 0, 2), void.reshape(fluid.shape[1:])


def solution(mesh):
    return jax.shard_map(
        on_device,
        mesh=mesh,
        in_specs=(
            P(None, "stream", "azim", None),
            P(("stream", "azim"), None, None),
            P(("stream", "azim")),
            P(("stream", "azim")),
            P(("stream", "azim")),
            P(("stream", "azim")),
        ),
        out_specs=(
            P(None, "stream", "azim", None),
            P(("stream", "azim"), None, None),
            P("stream", "azim", None),
        ),
        check_vma=False,
    )
```

```python
import functools

import jax
import jax.numpy as jnp
from jax import lax
from jax.experimental import pallas as pl
from jax.experimental.pallas import tpu as pltpu
from jax.sharding import PartitionSpec as P

SUBSTEPS = 8
TIME_STEP = 0.25
MEAN_FLOW = 0.5
DIFFUSION = 0.1
KERNEL_WIDTH = 1.5
GAS_INDEX = 4.2
PRESSURE_COUPLING = 0.3
AMBIENT = 1.0
RELAX_TIME = 0.5
VISCOUS = 0.08
SOURCE_GAIN = 0.05
VOID_SCALE = 0.01
FOUR_PI = 12.566370614359172
LOG2_E = 1.4426950408889634

CR = 128
BB = 128
NBLK = 512
COMPS = 5
CAP = 4
PACK = 24
GROUP = 8
STREAM_BLOCK = 32
VMEM_MIB = 58
FIRST_BATCH = 64
SECOND_BATCH = 32
CHUNK = 64
SHARP = 0.5 / (KERNEL_WIDTH * KERNEL_WIDTH) * LOG2_E
VMEM = pltpu.VMEM
SMEM = pltpu.SMEM


def split(values):
    high = values.astype(jnp.bfloat16)
    low = (values - high.astype(jnp.float32)).astype(jnp.bfloat16)
    return high, low


def centre_terms(position):
    centre = jnp.clip(jnp.floor(position + 0.5), 0.0, CR - 1.0)
    return centre * SHARP, 2.0 * position - centre


def raw_weights(cells, scaled_cells, near, far):
    return jnp.exp2((scaled_cells[...] - near) * (far - cells[...]))


def fill_cells(cells, scaled_cells):
    index = lax.broadcasted_iota(jnp.int32, (CR, BB), 0).astype(jnp.float32)
    cells[...] = index
    scaled_cells[...] = index * SHARP


def sample_phase(size, batches, positions, tile_of, flow_p, flow_v, rows_p, rows_v, cells, scaled_cells, sampled_p, sampled_v):
    sublane = lax.broadcasted_iota(jnp.int32, (GROUP, BB), 0)
    ones = jnp.ones((16, CR), jnp.bfloat16)

    def one(base):
        here = pl.ds(base, GROUP)
        near, far = centre_terms(positions(here))
        rows = jnp.concatenate([rows_p[here, :], rows_v[here, :]], axis=0)
        high, low = split(rows)
        left = jnp.concatenate([high, low, ones], axis=0)
        left = jnp.concatenate([left, left], axis=1)
        acc_p = jnp.zeros((GROUP, BB), jnp.float32)
        acc_v = acc_p
        acc_n = acc_p
        for i in range(0, GROUP, 2):
            right = jnp.concatenate(
                [
                    jnp.concatenate(
                        split(raw_weights(cells, scaled_cells, near[b : b + 1], far[b : b + 1])), axis=0
                    )
                    for b in (i, i + 1)
                ],
                axis=1,
            )
            both = jnp.dot(left, right, preferred_element_type=jnp.float32)
            for b, out in ((i, both[:, :BB]), (i + 1, both[:, BB:])):
                mine = sublane == b
                acc_p = jnp.where(mine, out[0:8] + out[16:24], acc_p)
                acc_v = jnp.where(mine, out[8:16] + out[24:32], acc_v)
                acc_n = jnp.where(mine, out[32:40], acc_n)
        sampled_p[here, :] = acc_p / acc_n
        sampled_v[here, :] = acc_v / acc_n

    def gather(base):
        for i in range(size):
            tile = tile_of(base + i)
            rows_p[pl.ds(base + i, 1), :] = flow_p[0, pl.ds(tile, 1), :]
            rows_v[pl.ds(base + i, 1), :] = flow_v[0, pl.ds(tile, 1), :]

    def body(batch, carry):
        for sub in range(size // GROUP):
            one(pl.multiple_of(batch * size + sub * GROUP, GROUP))
        gather(jnp.minimum(batch + 1, batches - 1) * size)
        return carry

    gather(0)
    lax.fori_loop(0, batches, body, 0)


def bubble_phase(chunks, component, state, sampled_p, sampled_v, source, void):
    h = TIME_STEP / SUBSTEPS

    def body(chunk, carry):
        here = pl.ds(pl.multiple_of(chunk * CHUNK, CHUNK), CHUNK)
        radius = component(0, here)
        growth = component(1, here)
        position = component(2, here)
        speed = component(3, here)
        rest_log = jnp.log2(component(4, here))
        drive = AMBIENT + PRESSURE_COUPLING * sampled_p[here, :]
        velocity = sampled_v[here, :]
        for _ in range(SUBSTEPS):
            inverse = 1.0 / radius
            gas = jnp.exp2(GAS_INDEX * (rest_log - jnp.log2(radius)))
            accel = (gas - drive - growth * (1.5 * growth + VISCOUS * inverse)) * inverse
            growth = growth + h * accel
            radius = radius + h * growth
            speed = speed + (h / RELAX_TIME) * (velocity - speed)
            position = position + h * speed
        state[here, 0, :] = radius
        state[here, 1, :] = growth
        state[here, 2, :] = position
        state[here, 3, :] = speed
        state[here, 4, :] = component(4, here)
        area = radius * radius
        source[here, :] = (SOURCE_GAIN * FOUR_PI) * area * growth
        if void is not None:
            void[here, :] = (VOID_SCALE * FOUR_PI / 3.0) * area * radius
        return carry

    lax.fori_loop(0, chunks, body, 0)


def spread_phase(size, batches, live_blocks, tile_of, state, amounts, cells, scaled_cells, grids, beside):
    sublane = lax.broadcasted_iota(jnp.int32, (GROUP, BB), 0)
    kinds = len(amounts)

    def one(base):
        here = pl.ds(base, GROUP)
        near, far = centre_terms(state[here, 2, :])
        whole = jnp.concatenate([a[here, :] for a in amounts], axis=0)
        accs = [jnp.zeros((GROUP, CR), jnp.float32) for _ in amounts]
        for i in range(0, GROUP, 2):
            lefts = []
            rights = []
            for b in (i, i + 1):
                w = raw_weights(cells, scaled_cells, near[b : b + 1], far[b : b + 1])
                total = jnp.sum(w, axis=0, keepdims=True)
                rights.append(jnp.concatenate(split(w), axis=1))
                left = jnp.concatenate(split(whole * (1.0 / total)), axis=0)
                lefts.append(jnp.concatenate([left, left], axis=1))
            left = jnp.concatenate(lefts, axis=0)
            right = jnp.concatenate(rights, axis=0)
            both = lax.dot_general(
                left, right, (((1,), (1,)), ((), ())), preferred_element_type=jnp.float32
            )
            for b in (0, 1):
                out = both[2 * GROUP * kinds * b :, CR * b : CR * (b + 1)]
                mine = sublane == i + b
                for kind in range(kinds):
                    lo = GROUP * kind
                    hi = GROUP * (kinds + kind)
                    accs[kind] = jnp.where(
                        mine, out[lo : lo + GROUP] + out[hi : hi + GROUP], accs[kind]
                    )
        alive = sublane + base < live_blocks
        accs = [jnp.where(alive, acc, 0.0) for acc in accs]
        return base, accs

    def body(batch, carry):
        done = [one(pl.multiple_of(batch * size + sub * GROUP, GROUP)) for sub in range(size // GROUP)]
        for base, accs in done:
            for i in range(GROUP):
                tile = tile_of(base + i)
                for grid, acc in zip(grids, accs):
                    grid[pl.ds(tile, 1), :] = grid[pl.ds(tile, 1), :] + acc[i : i + 1]
        beside(batch)
        return carry

    lax.fori_loop(0, batches, body, 0)


def first_bubbles_kernel(
    counts, order, tiles, bubbles, flow_p, flow_v, packed, source_grid,
    state, rows_p, rows_v, sampled_p, sampled_v, source, cells, scaled_cells,
):
    size = FIRST_BATCH
    live = counts[0]
    batches = (live + size - 1) // size
    chunks = (live + CHUNK - 1) // CHUNK
    fill_cells(cells, scaled_cells)
    source_grid[...] = jnp.zeros_like(source_grid)

    sample_phase(
        size, batches, lambda here: bubbles[2, here, :], lambda j: tiles[j], flow_p, flow_v, rows_p, rows_v,
        cells, scaled_cells, sampled_p, sampled_v,
    )
    bubble_phase(
        chunks, lambda c, here: bubbles[c, here, :], state, sampled_p, sampled_v, source, None
    )
    lane = lax.broadcasted_iota(jnp.int32, (PACK - COMPS * CAP, BB), 1)

    def pack(batch):
        for i in range(size // CAP):
            peer = batch * (size // CAP) + i
            flags = jnp.zeros((PACK - COMPS * CAP, BB), jnp.float32)
            for k in range(CAP):
                block = order[peer * CAP + k]
                alive = block < live
                packed[peer, COMPS * k : COMPS * (k + 1), :] = jnp.where(
                    alive, state[block, 0:COMPS, :], 0.0
                )
                flags = jnp.where((lane == k) & alive, 1.0, flags)
            packed[peer, COMPS * CAP : PACK, :] = flags

    def pack_rest(batch, carry):
        pack(batch)
        return carry

    spread_phase(
        size, batches, live, lambda j: tiles[j], state, [source], cells, scaled_cells, [source_grid], pack
    )
    lax.fori_loop(batches, NBLK // size, pack_rest, 0)


def second_bubbles_kernel(
    tiles, packed, flow_p, flow_v, bubbles_out, source_grid, void_grid,
    slots, flags, flag_sem, state, rows_p, rows_v, sampled_p, sampled_v, source, void, cells, scaled_cells,
):
    size = SECOND_BATCH
    copy = pltpu.make_async_copy(packed.at[:, COMPS * CAP, :], flags, flag_sem)
    copy.start()
    fill_cells(cells, scaled_cells)
    source_grid[...] = jnp.zeros_like(source_grid)
    void_grid[...] = jnp.zeros_like(void_grid)

    bubbles_out[...] = jnp.zeros_like(bubbles_out)
    copy.wait()

    def unpack(peer, live):
        for k in range(CAP):
            slot = peer * CAP + k
            state[live, 0:COMPS, :] = packed[peer, COMPS * k : COMPS * (k + 1), :]
            slots[live] = slot
            live = live + jnp.where(flags[peer, k] > 0.5, 1, 0)
        return live

    live = lax.fori_loop(0, NBLK // CAP, unpack, jnp.int32(0), unroll=4)
    last = slots[jnp.maximum(live - 1, 0)]
    for i in range(size):
        slots[live + i] = last
        state[jnp.minimum(live + i, NBLK - 1), 0:COMPS, :] = state[jnp.maximum(live - 1, 0), 0:COMPS, :]
    batches = (live + size - 1) // size
    chunks = (live + CHUNK - 1) // CHUNK

    sample_phase(
        size, batches, lambda here: state[here, 2, :], lambda j: tiles[slots[j]], flow_p, flow_v, rows_p, rows_v,
        cells, scaled_cells, sampled_p, sampled_v,
    )
    bubble_phase(
        chunks, lambda c, here: state[here, c, :], state, sampled_p, sampled_v, source, void
    )

    def put(batch):
        for i in range(size):
            j = batch * size + i
            slot = slots[j]
            for c in range(COMPS):
                bubbles_out[c, pl.ds(slot, 1), :] = state[j, c : c + 1, :]

    spread_phase(
        size, batches, live, lambda j: tiles[slots[j]], state, [source, void], cells, scaled_cells,
        [source_grid, void_grid], put,
    )


def fluid_kernel(
    flow, flow_before, flow_after, source, stream_before, stream_after, azim_before, azim_after, new, *faces
):
    step = pl.program_id(0)
    first, final = step == 0, step == pl.num_programs(0) - 1
    streams = flow.shape[1]
    azims = flow.shape[2]
    shape = (azims, CR)
    lane = lax.broadcasted_iota(jnp.int32, shape, 1)
    row = lax.broadcasted_iota(jnp.int32, shape, 0)
    first_lane, last_lane = lane == 0, lane == CR - 1
    first_row, last_row = row == 0, row == azims - 1
    a = 0.5 * TIME_STEP

    def plane(s, down, up):
        sums = []
        values = []
        stream_slope = []
        azim_slope = {}
        radial_slope = {}
        for c in range(4):
            f = flow[c, s]
            before = down(c)
            after = up(c)
            left = jnp.where(first_row, azim_before[c, pl.ds(s, 1), :], pltpu.roll(f, 1, 0))
            right = jnp.where(last_row, azim_after[c, pl.ds(s, 1), :], pltpu.roll(f, azims - 1, 0))
            inner = jnp.where(first_lane, 0.0, pltpu.roll(f, 1, 1))
            outer = jnp.where(last_lane, 0.0, pltpu.roll(f, CR - 1, 1))
            values.append(f)
            sums.append(((before + after) + (left + right)) + (inner + outer))
            stream_slope.append(after - before)
            if c in (0, 2):
                azim_slope[c] = right - left
            if c in (0, 3):
                radial_slope[c] = outer - inner
        rates = [
            MEAN_FLOW * stream_slope[0] + stream_slope[1] + azim_slope[2] + radial_slope[3],
            MEAN_FLOW * stream_slope[1] + stream_slope[0],
            MEAN_FLOW * stream_slope[2] + azim_slope[0],
            MEAN_FLOW * stream_slope[3] + radial_slope[0],
        ]
        for c in range(4):
            value = (1.0 - 6.0 * DIFFUSION) * values[c] + DIFFUSION * sums[c] - a * rates[c]
            if c == 0:
                value = value - TIME_STEP * source[s]
            new[c, s] = value
            if faces:
                faces[2][c, pl.ds(s, 1), :] = value[0:1]
                faces[3][c, pl.ds(s, 1), :] = value[azims - 1 : azims]

    for s in range(streams):
        plane(
            s,
            (lambda c: jnp.where(first, stream_before[c], flow_before[c, 0])) if s == 0 else (lambda c: flow[c, s - 1]),
            (lambda c: jnp.where(final, stream_after[c], flow_after[c, 0])) if s == streams - 1 else (lambda c: flow[c, s + 1]),
        )
    if faces:

        @pl.when(first)
        def _():
            faces[0][...] = new[:, 0]

        @pl.when(final)
        def _():
            faces[1][...] = new[:, streams - 1]


F32 = jnp.float32
SHAPE = jax.ShapeDtypeStruct


def whole(shape):
    return pl.BlockSpec(shape, lambda *_: (0,) * len(shape), memory_space=VMEM)


def component(c, tiles):
    return pl.BlockSpec((1, tiles, CR), lambda *_: (c, 0, 0), memory_space=VMEM)


def params():
    return pltpu.CompilerParams(vmem_limit_bytes=VMEM_MIB << 20)


def bubble_scratch(amounts):
    wide = [VMEM((NBLK, BB), F32)] * (4 + amounts)
    return [VMEM((NBLK, 8, BB), F32)] + wide + [VMEM((CR, BB), F32)] * 2


def first_bubbles(counts, order, tiles, bubbles, flow_rows):
    ntile = flow_rows.shape[1]
    peers = NBLK // CAP
    return pl.pallas_call(
        first_bubbles_kernel,
        grid=(1,),
        in_specs=[pl.BlockSpec(memory_space=SMEM)] * 3
        + [whole((COMPS, NBLK, BB)), component(0, ntile), component(3, ntile)],
        out_specs=[whole((peers, PACK, BB)), whole((ntile, CR))],
        out_shape=[SHAPE((peers, PACK, BB), F32), SHAPE((ntile, CR), F32)],
        scratch_shapes=bubble_scratch(1),
        compiler_params=params(),
        cost_estimate=pl.CostEstimate(flops=10**9, bytes_accessed=10**8, transcendentals=10**7),
        name="first_bubbles",
    )(counts, order, tiles, bubbles, flow_rows, flow_rows)


def second_bubbles(tiles, packed, flow_rows):
    ntile = flow_rows.shape[1]
    peers = NBLK // CAP
    return pl.pallas_call(
        second_bubbles_kernel,
        grid=(1,),
        in_specs=[pl.BlockSpec(memory_space=SMEM)]
        + [whole((peers, PACK, BB)), component(0, ntile), component(3, ntile)],
        out_specs=[whole((COMPS, NBLK, BB)), whole((ntile, CR)), whole((ntile, CR))],
        out_shape=[SHAPE((COMPS, NBLK, BB), F32), SHAPE((ntile, CR), F32), SHAPE((ntile, CR), F32)],
        scratch_shapes=[
            SMEM((NBLK + SECOND_BATCH,), jnp.int32),
            SMEM((peers, BB), F32),
            pltpu.SemaphoreType.DMA,
        ]
        + bubble_scratch(2),
        compiler_params=params(),
        cost_estimate=pl.CostEstimate(flops=10**9, bytes_accessed=10**8, transcendentals=10**7),
        name="second_bubbles",
    )(tiles, packed, flow_rows, flow_rows)


def fluid_update(flow, source, halos, with_faces):
    streams, azims = flow.shape[1:3]
    out_shape = [SHAPE(flow.shape, F32)]
    if with_faces:
        out_shape += [SHAPE((4, azims, CR), F32)] * 2 + [SHAPE((4, streams, CR), F32)] * 2
    slab = STREAM_BLOCK
    moving = pl.BlockSpec((4, slab, azims, CR), lambda i: (0, i, 0, 0))
    along = pl.BlockSpec((4, slab, CR), lambda i: (0, i, 0))
    fixed = pl.BlockSpec((4, azims, CR), lambda i: (0, 0, 0))
    return pl.pallas_call(
        fluid_kernel,
        grid=(streams // slab,),
        in_specs=[
            moving,
            pl.BlockSpec((4, 1, azims, CR), lambda i: (0, jnp.maximum(i * slab - 1, 0), 0, 0)),
            pl.BlockSpec((4, 1, azims, CR), lambda i: (0, jnp.minimum((i + 1) * slab, streams - 1), 0, 0)),
            pl.BlockSpec((slab, azims, CR), lambda i: (i, 0, 0)),
            fixed,
            fixed,
            along,
            along,
        ],
        out_specs=[moving, fixed, fixed, along, along] if with_faces else [moving],
        out_shape=out_shape,
        compiler_params=params(),
        cost_estimate=pl.CostEstimate(flops=10**8, bytes_accessed=3 * 10**7, transcendentals=0),
        name="fluid",
    )(flow, flow, flow, source.reshape(streams, azims, CR), *halos)


def exchange(head_stream, tail_stream, head_azim, tail_azim):
    streams = lax.axis_size("stream")
    azims = lax.axis_size("azim")
    return (
        lax.ppermute(tail_stream, "stream", [(i, i + 1) for i in range(streams - 1)]),
        lax.ppermute(head_stream, "stream", [(i + 1, i) for i in range(streams - 1)]),
        lax.ppermute(tail_azim, "azim", [(i, (i + 1) % azims) for i in range(azims)]),
        lax.ppermute(head_azim, "azim", [((i + 1) % azims, i) for i in range(azims)]),
    )


def on_device(fluid, bubbles, counts, outgoing_block_order, tiles_first_update, tiles_after):
    halos = exchange(fluid[:, 0], fluid[:, -1], fluid[:, :, 0], fluid[:, :, -1])
    rows = fluid.reshape(4, -1, CR)
    packed, source = first_bubbles(
        counts, outgoing_block_order, tiles_first_update, bubbles.transpose(1, 0, 2), rows
    )
    packed, halos = lax.optimization_barrier((packed, halos))
    arrived = lax.all_to_all(packed, ("stream", "azim"), split_axis=0, concat_axis=0, tiled=True)
    flow, *faces = fluid_update(fluid, source, halos, True)
    halos = exchange(*faces)
    moved, source, void = second_bubbles(tiles_after, arrived, flow.reshape(4, -1, CR))
    (flow,) = fluid_update(flow, source, halos, False)
    return flow, moved.transpose(1, 0, 2), void.reshape(fluid.shape[1:])


def solution(mesh):
    return jax.shard_map(
        on_device,
        mesh=mesh,
        in_specs=(
            P(None, "stream", "azim", None),
            P(("stream", "azim"), None, None),
            P(("stream", "azim")),
            P(("stream", "azim")),
            P(("stream", "azim")),
            P(("stream", "azim")),
        ),
        out_specs=(
            P(None, "stream", "azim", None),
            P(("stream", "azim"), None, None),
            P("stream", "azim", None),
        ),
        check_vma=False,
    )
```

```python
import functools

import jax
import jax.numpy as jnp
from jax import lax
from jax.experimental import pallas as pl
from jax.experimental.pallas import tpu as pltpu
from jax.sharding import PartitionSpec as P

SUBSTEPS = 8
TIME_STEP = 0.25
MEAN_FLOW = 0.5
DIFFUSION = 0.1
KERNEL_WIDTH = 1.5
GAS_INDEX = 4.2
PRESSURE_COUPLING = 0.3
AMBIENT = 1.0
RELAX_TIME = 0.5
VISCOUS = 0.08
SOURCE_GAIN = 0.05
VOID_SCALE = 0.01
FOUR_PI = 12.566370614359172
LOG2_E = 1.4426950408889634

CR = 128
BB = 128
NBLK = 512
COMPS = 5
CAP = 4
PACK = 24
GROUP = 8
STREAM_BLOCK = 32
VMEM_MIB = 58
FIRST_BATCH = 64
SECOND_BATCH = 32
CHUNK = 64
SHARP = 0.5 / (KERNEL_WIDTH * KERNEL_WIDTH) * LOG2_E
VMEM = pltpu.VMEM
SMEM = pltpu.SMEM


def split(values):
    high = values.astype(jnp.bfloat16)
    low = (values - high.astype(jnp.float32)).astype(jnp.bfloat16)
    return high, low


def centre_terms(position):
    centre = jnp.clip(jnp.floor(position + 0.5), 0.0, CR - 1.0)
    return centre * SHARP, 2.0 * position - centre


def raw_weights(cells, scaled_cells, near, far):
    return jnp.exp2((scaled_cells[...] - near) * (far - cells[...]))


def fill_cells(cells, scaled_cells):
    index = lax.broadcasted_iota(jnp.int32, (CR, BB), 0).astype(jnp.float32)
    cells[...] = index
    scaled_cells[...] = index * SHARP


def sample_phase(size, batches, positions, tile_of, flow_p, flow_v, rows_p, rows_v, cells, scaled_cells, sampled_p, sampled_v):
    sublane = lax.broadcasted_iota(jnp.int32, (GROUP, BB), 0)
    ones = jnp.ones((16, CR), jnp.bfloat16)

    def one(base):
        here = pl.ds(base, GROUP)
        near, far = centre_terms(positions(here))
        rows = jnp.concatenate([rows_p[here, :], rows_v[here, :]], axis=0)
        high, low = split(rows)
        left = jnp.concatenate([high, low, ones], axis=0)
        left = jnp.concatenate([left, left], axis=1)
        acc_p = jnp.zeros((GROUP, BB), jnp.float32)
        acc_v = acc_p
        acc_n = acc_p
        for i in range(0, GROUP, 2):
            right = jnp.concatenate(
                [
                    jnp.concatenate(
                        split(raw_weights(cells, scaled_cells, near[b : b + 1], far[b : b + 1])), axis=0
                    )
                    for b in (i, i + 1)
                ],
                axis=1,
            )
            both = jnp.dot(left, right, preferred_element_type=jnp.float32)
            for b, out in ((i, both[:, :BB]), (i + 1, both[:, BB:])):
                mine = sublane == b
                acc_p = jnp.where(mine, out[0:8] + out[16:24], acc_p)
                acc_v = jnp.where(mine, out[8:16] + out[24:32], acc_v)
                acc_n = jnp.where(mine, out[32:40], acc_n)
        sampled_p[here, :] = acc_p / acc_n
        sampled_v[here, :] = acc_v / acc_n

    def gather(base):
        for i in range(size):
            tile = tile_of(base + i)
            rows_p[pl.ds(base + i, 1), :] = flow_p[0, pl.ds(tile, 1), :]
            rows_v[pl.ds(base + i, 1), :] = flow_v[0, pl.ds(tile, 1), :]

    def body(batch, carry):
        for sub in range(size // GROUP):
            one(pl.multiple_of(batch * size + sub * GROUP, GROUP))
        gather(jnp.minimum(batch + 1, batches - 1) * size)
        return carry

    gather(0)
    lax.fori_loop(0, batches, body, 0)


def bubble_phase(chunks, component, state, sampled_p, sampled_v, places, source, void):
    h = TIME_STEP / SUBSTEPS

    def body(chunk, carry):
        here = pl.ds(pl.multiple_of(chunk * CHUNK, CHUNK), CHUNK)
        radius = component(0, here)
        growth = component(1, here)
        position = component(2, here)
        speed = component(3, here)
        rest_log = jnp.log2(component(4, here))
        drive = AMBIENT + PRESSURE_COUPLING * sampled_p[here, :]
        velocity = sampled_v[here, :]
        for _ in range(SUBSTEPS):
            inverse = 1.0 / radius
            gas = jnp.exp2(GAS_INDEX * (rest_log - jnp.log2(radius)))
            accel = (gas - drive - growth * (1.5 * growth + VISCOUS * inverse)) * inverse
            growth = growth + h * accel
            radius = radius + h * growth
            speed = speed + (h / RELAX_TIME) * (velocity - speed)
            position = position + h * speed
        state[here, 0, :] = radius
        state[here, 1, :] = growth
        state[here, 2, :] = position
        state[here, 3, :] = speed
        state[here, 4, :] = component(4, here)
        places[here, :] = position
        area = radius * radius
        source[here, :] = (SOURCE_GAIN * FOUR_PI) * area * growth
        if void is not None:
            void[here, :] = (VOID_SCALE * FOUR_PI / 3.0) * area * radius
        return carry

    lax.fori_loop(0, chunks, body, 0)


def spread_phase(size, batches, live_blocks, tile_of, places, amounts, cells, scaled_cells, grids, beside):
    sublane = lax.broadcasted_iota(jnp.int32, (GROUP, BB), 0)
    kinds = len(amounts)

    def one(base):
        here = pl.ds(base, GROUP)
        near, far = centre_terms(places[here, :])
        whole = jnp.concatenate([a[here, :] for a in amounts], axis=0)
        accs = [jnp.zeros((GROUP, CR), jnp.float32) for _ in amounts]
        for i in range(0, GROUP, 2):
            lefts = []
            rights = []
            for b in (i, i + 1):
                w = raw_weights(cells, scaled_cells, near[b : b + 1], far[b : b + 1])
                total = jnp.sum(w, axis=0, keepdims=True)
                rights.append(jnp.concatenate(split(w), axis=1))
                left = jnp.concatenate(split(whole * (1.0 / total)), axis=0)
                lefts.append(jnp.concatenate([left, left], axis=1))
            left = jnp.concatenate(lefts, axis=0)
            right = jnp.concatenate(rights, axis=0)
            both = lax.dot_general(
                left, right, (((1,), (1,)), ((), ())), preferred_element_type=jnp.float32
            )
            for b in (0, 1):
                out = both[2 * GROUP * kinds * b :, CR * b : CR * (b + 1)]
                mine = sublane == i + b
                for kind in range(kinds):
                    lo = GROUP * kind
                    hi = GROUP * (kinds + kind)
                    accs[kind] = jnp.where(
                        mine, out[lo : lo + GROUP] + out[hi : hi + GROUP], accs[kind]
                    )
        alive = sublane + base < live_blocks
        accs = [jnp.where(alive, acc, 0.0) for acc in accs]
        return base, accs

    def body(batch, carry):
        done = [one(pl.multiple_of(batch * size + sub * GROUP, GROUP)) for sub in range(size // GROUP)]
        for base, accs in done:
            for i in range(GROUP):
                tile = tile_of(base + i)
                for grid, acc in zip(grids, accs):
                    grid[pl.ds(tile, 1), :] = grid[pl.ds(tile, 1), :] + acc[i : i + 1]
        if beside is not None:
            beside(batch)
        return carry

    lax.fori_loop(0, batches, body, 0)


def first_bubbles_kernel(
    counts, order, tiles, bubbles, flow_p, flow_v, packed, places, source,
    state, rows_p, rows_v, sampled_p, sampled_v, cells, scaled_cells,
):
    size = FIRST_BATCH
    live = counts[0]
    batches = (live + size - 1) // size
    chunks = (live + CHUNK - 1) // CHUNK
    fill_cells(cells, scaled_cells)
    sample_phase(
        size, batches, lambda here: bubbles[2, here, :], lambda j: tiles[j], flow_p, flow_v, rows_p, rows_v,
        cells, scaled_cells, sampled_p, sampled_v,
    )
    bubble_phase(
        chunks, lambda c, here: bubbles[c, here, :], state, sampled_p, sampled_v, places, source, None
    )
    lane = lax.broadcasted_iota(jnp.int32, (PACK - COMPS * CAP, BB), 1)

    def pack(peer, carry):
        flags = jnp.zeros((PACK - COMPS * CAP, BB), jnp.float32)
        for k in range(CAP):
            block = order[peer * CAP + k]
            alive = block < live
            packed[peer, COMPS * k : COMPS * (k + 1), :] = jnp.where(
                alive, state[block, 0:COMPS, :], 0.0
            )
            flags = jnp.where((lane == k) & alive, 1.0, flags)
        packed[peer, COMPS * CAP : PACK, :] = flags
        return carry

    lax.fori_loop(0, NBLK // CAP, pack, 0, unroll=8)


def first_flow_kernel(
    counts, tiles, places, source, flow, flow_before, flow_after, stream_before, stream_after, azim_before,
    azim_after, new, face_0, face_1, face_2, face_3, source_grid, cells, scaled_cells,
):
    step = pl.program_id(0)

    @pl.when(step == 0)
    def _():
        size = FIRST_BATCH
        live = counts[0]
        fill_cells(cells, scaled_cells)
        source_grid[...] = jnp.zeros_like(source_grid)
        spread_phase(
            size, (live + size - 1) // size, live, lambda j: tiles[j], places, [source], cells, scaled_cells,
            [source_grid], None,
        )

    @pl.when(step > 0)
    def _():
        flow_slab(
            step - 1, pl.num_programs(0) - 1, flow, flow_before, flow_after, source_grid, stream_before,
            stream_after, azim_before, azim_after, new, face_0, face_1, face_2, face_3,
        )


def second_kernel(
    tiles, packed, flow_p, flow_v, flow, flow_before, flow_after, stream_before, stream_after, azim_before,
    azim_after, new, bubbles_out, void_grid, slots, flags, flag_sem, source_grid, places, source, void,
    *scratch,
):
    step = pl.program_id(0)

    @pl.when(step == 0)
    def _():
        second_bubbles(
            tiles, packed, flow_p, flow_v, bubbles_out, source_grid, void_grid, slots, flags, flag_sem,
            places, source, void, *scratch,
        )

    @pl.when(step > 0)
    def _():
        flow_slab(
            step - 1, pl.num_programs(0) - 1, flow, flow_before, flow_after, source_grid, stream_before,
            stream_after, azim_before, azim_after, new,
        )


def second_bubbles(
    tiles, packed, flow_p, flow_v, bubbles_out, source_grid, void_grid, slots, flags, flag_sem,
    places, source, void, state, rows_p, rows_v, sampled_p, sampled_v, cells, scaled_cells,
):
    size = SECOND_BATCH
    copy = pltpu.make_async_copy(packed.at[:, COMPS * CAP, :], flags, flag_sem)
    copy.start()
    fill_cells(cells, scaled_cells)
    source_grid[...] = jnp.zeros_like(source_grid)
    void_grid[...] = jnp.zeros_like(void_grid)

    bubbles_out[...] = jnp.zeros_like(bubbles_out)
    copy.wait()

    def unpack(peer, live):
        for k in range(CAP):
            slot = peer * CAP + k
            state[live, 0:COMPS, :] = packed[peer, COMPS * k : COMPS * (k + 1), :]
            slots[live] = slot
            live = live + jnp.where(flags[peer, k] > 0.5, 1, 0)
        return live

    live = lax.fori_loop(0, NBLK // CAP, unpack, jnp.int32(0), unroll=4)
    last = slots[jnp.maximum(live - 1, 0)]
    for i in range(size):
        slots[live + i] = last
        state[jnp.minimum(live + i, NBLK - 1), 0:COMPS, :] = state[jnp.maximum(live - 1, 0), 0:COMPS, :]
    batches = (live + size - 1) // size
    chunks = (live + CHUNK - 1) // CHUNK

    sample_phase(
        size, batches, lambda here: state[here, 2, :], lambda j: tiles[slots[j]], flow_p, flow_v, rows_p, rows_v,
        cells, scaled_cells, sampled_p, sampled_v,
    )
    bubble_phase(
        chunks, lambda c, here: state[here, c, :], state, sampled_p, sampled_v, places, source, void
    )

    def put(batch):
        for i in range(size):
            j = batch * size + i
            slot = slots[j]
            for c in range(COMPS):
                bubbles_out[c, pl.ds(slot, 1), :] = state[j, c : c + 1, :]

    spread_phase(
        size, batches, live, lambda j: tiles[slots[j]], places, [source, void], cells, scaled_cells,
        [source_grid, void_grid], put,
    )


def flow_slab(
    index, slabs, flow, flow_before, flow_after, source, stream_before, stream_after, azim_before,
    azim_after, new, *faces,
):
    first, final = index == 0, index == slabs - 1
    streams = flow.shape[1]
    azims = flow.shape[2]
    shape = (azims, CR)
    lane = lax.broadcasted_iota(jnp.int32, shape, 1)
    row = lax.broadcasted_iota(jnp.int32, shape, 0)
    first_lane, last_lane = lane == 0, lane == CR - 1
    first_row, last_row = row == 0, row == azims - 1
    a = 0.5 * TIME_STEP

    def plane(s, down, up):
        sums = []
        values = []
        stream_slope = []
        azim_slope = {}
        radial_slope = {}
        for c in range(4):
            f = flow[c, s]
            before = down(c)
            after = up(c)
            left = jnp.where(first_row, azim_before[c, pl.ds(s, 1), :], pltpu.roll(f, 1, 0))
            right = jnp.where(last_row, azim_after[c, pl.ds(s, 1), :], pltpu.roll(f, azims - 1, 0))
            inner = jnp.where(first_lane, 0.0, pltpu.roll(f, 1, 1))
            outer = jnp.where(last_lane, 0.0, pltpu.roll(f, CR - 1, 1))
            values.append(f)
            sums.append(((before + after) + (left + right)) + (inner + outer))
            stream_slope.append(after - before)
            if c in (0, 2):
                azim_slope[c] = right - left
            if c in (0, 3):
                radial_slope[c] = outer - inner
        rates = [
            MEAN_FLOW * stream_slope[0] + stream_slope[1] + azim_slope[2] + radial_slope[3],
            MEAN_FLOW * stream_slope[1] + stream_slope[0],
            MEAN_FLOW * stream_slope[2] + azim_slope[0],
            MEAN_FLOW * stream_slope[3] + radial_slope[0],
        ]
        for c in range(4):
            value = (1.0 - 6.0 * DIFFUSION) * values[c] + DIFFUSION * sums[c] - a * rates[c]
            if c == 0:
                value = value - TIME_STEP * source[pl.ds(pl.multiple_of((index * streams + s) * azims, azims), azims), :]
            new[c, s] = value
            if faces:
                faces[2][c, pl.ds(s, 1), :] = value[0:1]
                faces[3][c, pl.ds(s, 1), :] = value[azims - 1 : azims]

    for s in range(streams):
        plane(
            s,
            (lambda c: jnp.where(first, stream_before[c], flow_before[c, 0])) if s == 0 else (lambda c: flow[c, s - 1]),
            (lambda c: jnp.where(final, stream_after[c], flow_after[c, 0])) if s == streams - 1 else (lambda c: flow[c, s + 1]),
        )
    if faces:

        @pl.when(first)
        def _():
            faces[0][...] = new[:, 0]

        @pl.when(final)
        def _():
            faces[1][...] = new[:, streams - 1]


F32 = jnp.float32
SHAPE = jax.ShapeDtypeStruct


def whole(shape):
    return pl.BlockSpec(shape, lambda *_: (0,) * len(shape), memory_space=VMEM)


def component(c, tiles):
    return pl.BlockSpec((1, tiles, CR), lambda *_: (c, 0, 0), memory_space=VMEM)


def params():
    return pltpu.CompilerParams(vmem_limit_bytes=VMEM_MIB << 20)


def bubble_scratch():
    return [VMEM((NBLK, 8, BB), F32)] + [VMEM((NBLK, BB), F32)] * 4 + [VMEM((CR, BB), F32)] * 2


def first_bubbles(counts, order, tiles, bubbles, flow_rows):
    ntile = flow_rows.shape[1]
    peers = NBLK // CAP
    return pl.pallas_call(
        first_bubbles_kernel,
        grid=(1,),
        in_specs=[pl.BlockSpec(memory_space=SMEM)] * 3
        + [whole((COMPS, NBLK, BB)), component(0, ntile), component(3, ntile)],
        out_specs=[whole((peers, PACK, BB))] + [whole((NBLK, BB))] * 2,
        out_shape=[SHAPE((peers, PACK, BB), F32)] + [SHAPE((NBLK, BB), F32)] * 2,
        scratch_shapes=bubble_scratch(),
        compiler_params=params(),
        cost_estimate=pl.CostEstimate(flops=10**9, bytes_accessed=10**8, transcendentals=10**7),
        name="first_bubbles",
    )(counts, order, tiles, bubbles, flow_rows, flow_rows)


def slab_specs(streams, azims):
    slab = STREAM_BLOCK
    moving = pl.BlockSpec((4, slab, azims, CR), lambda i: (0, jnp.maximum(i - 1, 0), 0, 0))
    before = pl.BlockSpec((4, 1, azims, CR), lambda i: (0, jnp.maximum((i - 1) * slab - 1, 0), 0, 0))
    after = pl.BlockSpec(
        (4, 1, azims, CR), lambda i: (0, jnp.minimum(jnp.maximum(i, 1) * slab, streams - 1), 0, 0)
    )
    along = pl.BlockSpec((4, slab, CR), lambda i: (0, jnp.maximum(i - 1, 0), 0))
    fixed = whole((4, azims, CR))
    return (1 + streams // slab,), [moving, before, after, fixed, fixed, along, along], moving, along, fixed


def first_flow(counts, tiles, places, source, flow, halos):
    streams, azims = flow.shape[1:3]
    grid, slabs, moving, along, fixed = slab_specs(streams, azims)
    return pl.pallas_call(
        first_flow_kernel,
        grid=grid,
        in_specs=[pl.BlockSpec(memory_space=SMEM)] * 2 + [whole((NBLK, BB))] * 2 + slabs,
        out_specs=[moving, fixed, fixed, along, along],
        out_shape=[SHAPE(flow.shape, F32)]
        + [SHAPE((4, azims, CR), F32)] * 2
        + [SHAPE((4, streams, CR), F32)] * 2,
        scratch_shapes=[VMEM((streams * azims, CR), F32)] + [VMEM((CR, BB), F32)] * 2,
        compiler_params=params(),
        cost_estimate=pl.CostEstimate(flops=10**9, bytes_accessed=8 * 10**7, transcendentals=10**7),
        name="first_flow",
    )(counts, tiles, places, source, flow, flow, flow, *halos)


def second_update(tiles, packed, flow, halos):
    streams, azims = flow.shape[1:3]
    grid, slabs, moving, along, fixed = slab_specs(streams, azims)
    ntile = streams * azims
    peers = NBLK // CAP
    rows = flow.reshape(4, ntile, CR)
    return pl.pallas_call(
        second_kernel,
        grid=grid,
        in_specs=[pl.BlockSpec(memory_space=SMEM)]
        + [whole((peers, PACK, BB)), component(0, ntile), component(3, ntile)]
        + slabs,
        out_specs=[moving, whole((COMPS, NBLK, BB)), whole((ntile, CR))],
        out_shape=[SHAPE(flow.shape, F32), SHAPE((COMPS, NBLK, BB), F32), SHAPE((ntile, CR), F32)],
        scratch_shapes=[
            SMEM((NBLK + SECOND_BATCH,), jnp.int32),
            SMEM((peers, BB), F32),
            pltpu.SemaphoreType.DMA,
            VMEM((ntile, CR), F32),
        ]
        + [VMEM((NBLK, BB), F32)] * 3
        + bubble_scratch(),
        compiler_params=params(),
        cost_estimate=pl.CostEstimate(flops=10**9, bytes_accessed=10**8, transcendentals=10**7),
        name="second_update",
    )(tiles, packed, rows, rows, flow, flow, flow, *halos)


def exchange(head_stream, tail_stream, head_azim, tail_azim):
    streams = lax.axis_size("stream")
    azims = lax.axis_size("azim")
    return (
        lax.ppermute(tail_stream, "stream", [(i, i + 1) for i in range(streams - 1)]),
        lax.ppermute(head_stream, "stream", [(i + 1, i) for i in range(streams - 1)]),
        lax.ppermute(tail_azim, "azim", [(i, (i + 1) % azims) for i in range(azims)]),
        lax.ppermute(head_azim, "azim", [((i + 1) % azims, i) for i in range(azims)]),
    )


def on_device(fluid, bubbles, counts, outgoing_block_order, tiles_first_update, tiles_after):
    halos = exchange(fluid[:, 0], fluid[:, -1], fluid[:, :, 0], fluid[:, :, -1])
    rows = fluid.reshape(4, -1, CR)
    packed, places, source = first_bubbles(
        counts, outgoing_block_order, tiles_first_update, bubbles.transpose(1, 0, 2), rows
    )
    packed, halos = lax.optimization_barrier((packed, halos))
    arrived = lax.all_to_all(packed, ("stream", "azim"), split_axis=0, concat_axis=0, tiled=True)
    flow, *faces = first_flow(counts, tiles_first_update, places, source, fluid, halos)
    flow, moved, void = second_update(tiles_after, arrived, flow, exchange(*faces))
    return flow, moved.transpose(1, 0, 2), void.reshape(fluid.shape[1:])


def solution(mesh):
    return jax.shard_map(
        on_device,
        mesh=mesh,
        in_specs=(
            P(None, "stream", "azim", None),
            P(("stream", "azim"), None, None),
            P(("stream", "azim")),
            P(("stream", "azim")),
            P(("stream", "azim")),
            P(("stream", "azim")),
        ),
        out_specs=(
            P(None, "stream", "azim", None),
            P(("stream", "azim"), None, None),
            P("stream", "azim", None),
        ),
        check_vma=False,
    )
```

```python
import functools

import jax
import jax.numpy as jnp
from jax import lax
from jax.experimental import pallas as pl
from jax.experimental.pallas import tpu as pltpu
from jax.sharding import PartitionSpec as P

SUBSTEPS = 8
TIME_STEP = 0.25
MEAN_FLOW = 0.5
DIFFUSION = 0.1
KERNEL_WIDTH = 1.5
GAS_INDEX = 4.2
PRESSURE_COUPLING = 0.3
AMBIENT = 1.0
RELAX_TIME = 0.5
VISCOUS = 0.08
SOURCE_GAIN = 0.05
VOID_SCALE = 0.01
FOUR_PI = 12.566370614359172
LOG2_E = 1.4426950408889634

CR = 128
BB = 128
NBLK = 512
COMPS = 5
CAP = 4
PACK = 24
GROUP = 8
AZIMS = 32
SLAB = 8
VMEM_MIB = 58
FIRST_BATCH = 64
SECOND_BATCH = 32
CHUNK = 64
SHARP = 0.5 / (KERNEL_WIDTH * KERNEL_WIDTH) * LOG2_E
VMEM = pltpu.VMEM
SMEM = pltpu.SMEM
ANY = pl.BlockSpec(memory_space=pl.ANY)


def split(values):
    high = values.astype(jnp.bfloat16)
    low = (values - high.astype(jnp.float32)).astype(jnp.bfloat16)
    return high, low


def centre_terms(position):
    centre = jnp.clip(jnp.floor(position + 0.5), 0.0, CR - 1.0)
    return centre * SHARP, 2.0 * position - centre


def raw_weights(cells, scaled_cells, near, far):
    return jnp.exp2((scaled_cells[...] - near) * (far - cells[...]))


def fill_cells(cells, scaled_cells):
    index = lax.broadcasted_iota(jnp.int32, (CR, BB), 0).astype(jnp.float32)
    cells[...] = index
    scaled_cells[...] = index * SHARP


def sample_phase(size, batches, positions, tile_of, row_of, rows_p, rows_v, cells, scaled_cells, sampled_p, sampled_v):
    sublane = lax.broadcasted_iota(jnp.int32, (GROUP, BB), 0)
    ones = jnp.ones((16, CR), jnp.bfloat16)

    def one(base):
        here = pl.ds(base, GROUP)
        near, far = centre_terms(positions(here))
        rows = jnp.concatenate([rows_p[here, :], rows_v[here, :]], axis=0)
        high, low = split(rows)
        left = jnp.concatenate([high, low, ones], axis=0)
        left = jnp.concatenate([left, left], axis=1)
        acc_p = jnp.zeros((GROUP, BB), jnp.float32)
        acc_v = acc_p
        acc_n = acc_p
        for i in range(0, GROUP, 2):
            right = jnp.concatenate(
                [
                    jnp.concatenate(
                        split(raw_weights(cells, scaled_cells, near[b : b + 1], far[b : b + 1])), axis=0
                    )
                    for b in (i, i + 1)
                ],
                axis=1,
            )
            both = jnp.dot(left, right, preferred_element_type=jnp.float32)
            for b, out in ((i, both[:, :BB]), (i + 1, both[:, BB:])):
                mine = sublane == b
                acc_p = jnp.where(mine, out[0:8] + out[16:24], acc_p)
                acc_v = jnp.where(mine, out[8:16] + out[24:32], acc_v)
                acc_n = jnp.where(mine, out[32:40], acc_n)
        sampled_p[here, :] = acc_p / acc_n
        sampled_v[here, :] = acc_v / acc_n

    def gather(base):
        for i in range(size):
            tile = tile_of(base + i)
            rows_p[pl.ds(base + i, 1), :] = row_of(0, tile)
            rows_v[pl.ds(base + i, 1), :] = row_of(3, tile)

    def body(batch, carry):
        for sub in range(size // GROUP):
            one(pl.multiple_of(batch * size + sub * GROUP, GROUP))
        gather(jnp.minimum(batch + 1, batches - 1) * size)
        return carry

    gather(0)
    lax.fori_loop(0, batches, body, 0)


def bubble_phase(chunks, component, state, sampled_p, sampled_v, places, source, void):
    h = TIME_STEP / SUBSTEPS

    def body(chunk, carry):
        here = pl.ds(pl.multiple_of(chunk * CHUNK, CHUNK), CHUNK)
        radius = component(0, here)
        growth = component(1, here)
        position = component(2, here)
        speed = component(3, here)
        rest_log = jnp.log2(component(4, here))
        drive = AMBIENT + PRESSURE_COUPLING * sampled_p[here, :]
        velocity = sampled_v[here, :]
        for _ in range(SUBSTEPS):
            inverse = 1.0 / radius
            gas = jnp.exp2(GAS_INDEX * (rest_log - jnp.log2(radius)))
            accel = (gas - drive - growth * (1.5 * growth + VISCOUS * inverse)) * inverse
            growth = growth + h * accel
            radius = radius + h * growth
            speed = speed + (h / RELAX_TIME) * (velocity - speed)
            position = position + h * speed
        state[here, 0, :] = radius
        state[here, 1, :] = growth
        state[here, 2, :] = position
        state[here, 3, :] = speed
        state[here, 4, :] = component(4, here)
        places[here, :] = position
        area = radius * radius
        source[here, :] = (SOURCE_GAIN * FOUR_PI) * area * growth
        if void is not None:
            void[here, :] = (VOID_SCALE * FOUR_PI / 3.0) * area * radius
        return carry

    lax.fori_loop(0, chunks, body, 0)


def spread_phase(size, batches, live_blocks, tile_of, places, amounts, cells, scaled_cells, grids, beside):
    sublane = lax.broadcasted_iota(jnp.int32, (GROUP, BB), 0)
    kinds = len(amounts)

    def one(base):
        here = pl.ds(base, GROUP)
        near, far = centre_terms(places[here, :])
        whole = jnp.concatenate([a[here, :] for a in amounts], axis=0)
        accs = [jnp.zeros((GROUP, CR), jnp.float32) for _ in amounts]
        for i in range(0, GROUP, 2):
            lefts = []
            rights = []
            for b in (i, i + 1):
                w = raw_weights(cells, scaled_cells, near[b : b + 1], far[b : b + 1])
                total = jnp.sum(w, axis=0, keepdims=True)
                rights.append(jnp.concatenate(split(w), axis=1))
                left = jnp.concatenate(split(whole * (1.0 / total)), axis=0)
                lefts.append(jnp.concatenate([left, left], axis=1))
            left = jnp.concatenate(lefts, axis=0)
            right = jnp.concatenate(rights, axis=0)
            both = lax.dot_general(
                left, right, (((1,), (1,)), ((), ())), preferred_element_type=jnp.float32
            )
            for b in (0, 1):
                out = both[2 * GROUP * kinds * b :, CR * b : CR * (b + 1)]
                mine = sublane == i + b
                for kind in range(kinds):
                    lo = GROUP * kind
                    hi = GROUP * (kinds + kind)
                    accs[kind] = jnp.where(
                        mine, out[lo : lo + GROUP] + out[hi : hi + GROUP], accs[kind]
                    )
        alive = sublane + base < live_blocks
        accs = [jnp.where(alive, acc, 0.0) for acc in accs]
        return base, accs

    def body(batch, carry):
        done = [one(pl.multiple_of(batch * size + sub * GROUP, GROUP)) for sub in range(size // GROUP)]
        for base, accs in done:
            for i in range(GROUP):
                tile = tile_of(base + i)
                for grid, acc in zip(grids, accs):
                    grid[pl.ds(tile, 1), :] = grid[pl.ds(tile, 1), :] + acc[i : i + 1]
        if beside is not None:
            beside(batch)
        return carry

    lax.fori_loop(0, batches, body, 0)


def first_bubbles_kernel(
    counts, order, tiles, bubbles, flow_p, flow_v, packed, places, source,
    state, rows_p, rows_v, sampled_p, sampled_v, cells, scaled_cells,
):
    size = FIRST_BATCH
    live = counts[0]
    batches = (live + size - 1) // size
    chunks = (live + CHUNK - 1) // CHUNK
    fill_cells(cells, scaled_cells)
    sample_phase(
        size, batches, lambda here: bubbles[2, here, :], lambda j: tiles[j],
        lambda c, tile: (flow_v if c else flow_p)[0, pl.ds(tile, 1), :], rows_p, rows_v,
        cells, scaled_cells, sampled_p, sampled_v,
    )
    bubble_phase(
        chunks, lambda c, here: bubbles[c, here, :], state, sampled_p, sampled_v, places, source, None
    )
    lane = lax.broadcasted_iota(jnp.int32, (PACK - COMPS * CAP, BB), 1)

    def pack(peer, carry):
        flags = jnp.zeros((PACK - COMPS * CAP, BB), jnp.float32)
        for k in range(CAP):
            block = order[peer * CAP + k]
            alive = block < live
            packed[peer, COMPS * k : COMPS * (k + 1), :] = jnp.where(
                alive, state[block, 0:COMPS, :], 0.0
            )
            flags = jnp.where((lane == k) & alive, 1.0, flags)
        packed[peer, COMPS * CAP : PACK, :] = flags
        return carry

    lax.fori_loop(0, NBLK // CAP, pack, 0, unroll=8)


def first_flow_kernel(
    counts, tiles, places, source, flow_in, stream_before, stream_after, azim_before, azim_after,
    new_out, face_0, face_1, face_2, face_3, flow, new, in_sems, out_sems, source_grid, cells, scaled_cells,
):
    copies = flow_copies(flow_in, stream_before, stream_after, flow, in_sems)
    for copy in copies:
        copy.start()
    size = FIRST_BATCH
    live = counts[0]
    fill_cells(cells, scaled_cells)
    source_grid[...] = jnp.zeros_like(source_grid)
    spread_phase(
        size, (live + size - 1) // size, live, lambda j: tiles[j], places, [source], cells, scaled_cells,
        [source_grid], None,
    )
    for copy in copies:
        copy.wait()
    flow_update(flow, source_grid, azim_before, azim_after, new, new_out, out_sems, face_2, face_3)
    streams = new.shape[1] // AZIMS
    face_0[...] = new[:, 0:AZIMS, :]
    face_1[...] = new[:, (streams - 1) * AZIMS :, :]
    flow_stored(new, new_out, out_sems)


def second_kernel(
    tiles, packed, flow_in, stream_before, stream_after, azim_before, azim_after,
    new_out, moved_out, void_out,
    flow, new, in_sems, out_sems, source_grid, void_grid, bubbles_out, moved_sem, void_sem,
    slots, flags, flag_sem, places, source, void,
    state, rows_p, rows_v, sampled_p, sampled_v, cells, scaled_cells,
):
    copies = flow_copies(flow_in, stream_before, stream_after, flow, in_sems)
    for copy in copies:
        copy.start()
    size = SECOND_BATCH
    copy = pltpu.make_async_copy(packed.at[:, COMPS * CAP, :], flags, flag_sem)
    copy.start()
    fill_cells(cells, scaled_cells)
    source_grid[...] = jnp.zeros_like(source_grid)
    void_grid[...] = jnp.zeros_like(void_grid)

    bubbles_out[...] = jnp.zeros_like(bubbles_out)
    copy.wait()

    def unpack(peer, live):
        for k in range(CAP):
            slot = peer * CAP + k
            state[live, 0:COMPS, :] = packed[peer, COMPS * k : COMPS * (k + 1), :]
            slots[live] = slot
            live = live + jnp.where(flags[peer, k] > 0.5, 1, 0)
        return live

    live = lax.fori_loop(0, NBLK // CAP, unpack, jnp.int32(0), unroll=4)
    last = slots[jnp.maximum(live - 1, 0)]
    for i in range(size):
        slots[live + i] = last
        state[jnp.minimum(live + i, NBLK - 1), 0:COMPS, :] = state[jnp.maximum(live - 1, 0), 0:COMPS, :]
    batches = (live + size - 1) // size
    chunks = (live + CHUNK - 1) // CHUNK
    for copy in copies[:2]:
        copy.wait()
    sample_phase(
        size, batches, lambda here: state[here, 2, :], lambda j: tiles[slots[j]],
        lambda c, tile: flow[c, pl.ds(tile + AZIMS, 1), :], rows_p, rows_v,
        cells, scaled_cells, sampled_p, sampled_v,
    )
    bubble_phase(
        chunks, lambda c, here: state[here, c, :], state, sampled_p, sampled_v, places, source, void
    )

    def put(batch):
        for i in range(size):
            j = batch * size + i
            slot = slots[j]
            for c in range(COMPS):
                bubbles_out[c, pl.ds(slot, 1), :] = state[j, c : c + 1, :]

    spread_phase(
        size, batches, live, lambda j: tiles[slots[j]], places, [source, void], cells, scaled_cells,
        [source_grid, void_grid], put,
    )
    moved_copy = pltpu.make_async_copy(bubbles_out, moved_out, moved_sem)
    void_copy = pltpu.make_async_copy(void_grid, void_out, void_sem)
    moved_copy.start()
    void_copy.start()
    for copy in copies[2:]:
        copy.wait()
    flow_update(flow, source_grid, azim_before, azim_after, new, new_out, out_sems)
    moved_copy.wait()
    void_copy.wait()
    flow_stored(new, new_out, out_sems)


def flow_copies(flow_in, stream_before, stream_after, flow, sems):
    tiles = flow_in.shape[1]
    parts = [(flow_in.at[c], flow.at[c, AZIMS : AZIMS + tiles]) for c in (0, 3, 1, 2)]
    parts.append((stream_before, flow.at[:, 0:AZIMS]))
    parts.append((stream_after, flow.at[:, AZIMS + tiles : AZIMS + tiles + AZIMS]))
    return [pltpu.make_async_copy(src, dst, sems.at[i]) for i, (src, dst) in enumerate(parts)]


def slab_copy(slab, new, new_out, sems):
    here = pl.ds(pl.multiple_of(slab * SLAB * AZIMS, SLAB * AZIMS), SLAB * AZIMS)
    return pltpu.make_async_copy(new.at[:, here], new_out.at[:, here], sems.at[slab])


def flow_stored(new, new_out, sems):
    for slab in range(new.shape[1] // AZIMS // SLAB):
        slab_copy(slab, new, new_out, sems).wait()


def flow_update(flow, source, azim_before, azim_after, new, new_out, sems, *faces):
    shape = (AZIMS, CR)
    lane = lax.broadcasted_iota(jnp.int32, shape, 1)
    row = lax.broadcasted_iota(jnp.int32, shape, 0)
    first_lane, last_lane = lane == 0, lane == CR - 1
    first_row, last_row = row == 0, row == AZIMS - 1
    a = 0.5 * TIME_STEP

    def plane(s):
        start = pl.multiple_of(s * AZIMS, AZIMS)
        here = pl.ds(start, AZIMS)
        sums = []
        values = []
        stream_slope = []
        azim_slope = {}
        radial_slope = {}
        for c in range(4):
            before = flow[c, here, :]
            f = flow[c, pl.ds(start + AZIMS, AZIMS), :]
            after = flow[c, pl.ds(start + 2 * AZIMS, AZIMS), :]
            left = jnp.where(first_row, azim_before[c, pl.ds(s, 1), :], pltpu.roll(f, 1, 0))
            right = jnp.where(last_row, azim_after[c, pl.ds(s, 1), :], pltpu.roll(f, AZIMS - 1, 0))
            inner = jnp.where(first_lane, 0.0, pltpu.roll(f, 1, 1))
            outer = jnp.where(last_lane, 0.0, pltpu.roll(f, CR - 1, 1))
            values.append(f)
            sums.append(((before + after) + (left + right)) + (inner + outer))
            stream_slope.append(after - before)
            if c in (0, 2):
                azim_slope[c] = right - left
            if c in (0, 3):
                radial_slope[c] = outer - inner
        rates = [
            MEAN_FLOW * stream_slope[0] + stream_slope[1] + azim_slope[2] + radial_slope[3],
            MEAN_FLOW * stream_slope[1] + stream_slope[0],
            MEAN_FLOW * stream_slope[2] + azim_slope[0],
            MEAN_FLOW * stream_slope[3] + radial_slope[0],
        ]
        for c in range(4):
            value = (1.0 - 6.0 * DIFFUSION) * values[c] + DIFFUSION * sums[c] - a * rates[c]
            if c == 0:
                value = value - TIME_STEP * source[here, :]
            new[c, here, :] = value
            if faces:
                faces[0][c, pl.ds(s, 1), :] = value[0:1]
                faces[1][c, pl.ds(s, 1), :] = value[AZIMS - 1 : AZIMS]

    def body(slab, carry):
        for i in range(SLAB):
            plane(slab * SLAB + i)
        slab_copy(slab, new, new_out, sems).start()
        return carry

    lax.fori_loop(0, new.shape[1] // AZIMS // SLAB, body, 0)


F32 = jnp.float32
SHAPE = jax.ShapeDtypeStruct


def whole(shape):
    return pl.BlockSpec(shape, lambda *_: (0,) * len(shape), memory_space=VMEM)


def component(c, tiles):
    return pl.BlockSpec((1, tiles, CR), lambda *_: (c, 0, 0), memory_space=VMEM)


def params():
    return pltpu.CompilerParams(vmem_limit_bytes=VMEM_MIB << 20)


def bubble_scratch():
    return [VMEM((NBLK, 8, BB), F32)] + [VMEM((NBLK, BB), F32)] * 4 + [VMEM((CR, BB), F32)] * 2


def first_bubbles(counts, order, tiles, bubbles, flow_rows):
    ntile = flow_rows.shape[1]
    peers = NBLK // CAP
    return pl.pallas_call(
        first_bubbles_kernel,
        grid=(1,),
        in_specs=[pl.BlockSpec(memory_space=SMEM)] * 3
        + [whole((COMPS, NBLK, BB)), component(0, ntile), component(3, ntile)],
        out_specs=[whole((peers, PACK, BB))] + [whole((NBLK, BB))] * 2,
        out_shape=[SHAPE((peers, PACK, BB), F32)] + [SHAPE((NBLK, BB), F32)] * 2,
        scratch_shapes=bubble_scratch(),
        compiler_params=params(),
        cost_estimate=pl.CostEstimate(flops=10**9, bytes_accessed=10**8, transcendentals=10**7),
        name="first_bubbles",
    )(counts, order, tiles, bubbles, flow_rows, flow_rows)


def flow_scratch(streams):
    return [
        VMEM((4, (streams + 2) * AZIMS, CR), F32),
        VMEM((4, streams * AZIMS, CR), F32),
        pltpu.SemaphoreType.DMA((6,)),
        pltpu.SemaphoreType.DMA((streams // SLAB,)),
        VMEM((streams * AZIMS, CR), F32),
    ]


def flow_specs(streams):
    return [ANY] * 3 + [whole((4, streams, CR))] * 2


def first_flow(counts, tiles, places, source, flow, halos):
    streams = flow.shape[1] // AZIMS
    return pl.pallas_call(
        first_flow_kernel,
        grid=(1,),
        in_specs=[pl.BlockSpec(memory_space=SMEM)] * 2 + [whole((NBLK, BB))] * 2 + flow_specs(streams),
        out_specs=[ANY] + [whole((4, AZIMS, CR))] * 2 + [whole((4, streams, CR))] * 2,
        out_shape=[SHAPE(flow.shape, F32)]
        + [SHAPE((4, AZIMS, CR), F32)] * 2
        + [SHAPE((4, streams, CR), F32)] * 2,
        scratch_shapes=flow_scratch(streams) + [VMEM((CR, BB), F32)] * 2,
        compiler_params=params(),
        cost_estimate=pl.CostEstimate(flops=10**9, bytes_accessed=8 * 10**7, transcendentals=10**7),
        name="first_flow",
    )(counts, tiles, places, source, flow, *halos)


def second_update(tiles, packed, flow, halos):
    ntile = flow.shape[1]
    streams = ntile // AZIMS
    peers = NBLK // CAP
    return pl.pallas_call(
        second_kernel,
        grid=(1,),
        in_specs=[pl.BlockSpec(memory_space=SMEM), whole((peers, PACK, BB))] + flow_specs(streams),
        out_specs=[ANY] * 3,
        out_shape=[SHAPE(flow.shape, F32), SHAPE((COMPS, NBLK, BB), F32), SHAPE((ntile, CR), F32)],
        scratch_shapes=flow_scratch(streams)
        + [
            VMEM((ntile, CR), F32),
            VMEM((COMPS, NBLK, BB), F32),
            pltpu.SemaphoreType.DMA,
            pltpu.SemaphoreType.DMA,
            SMEM((NBLK + SECOND_BATCH,), jnp.int32),
            SMEM((peers, BB), F32),
            pltpu.SemaphoreType.DMA,
        ]
        + [VMEM((NBLK, BB), F32)] * 3
        + bubble_scratch(),
        compiler_params=params(),
        cost_estimate=pl.CostEstimate(flops=10**9, bytes_accessed=10**8, transcendentals=10**7),
        name="second_update",
    )(tiles, packed, flow, *halos)


def exchange(head_stream, tail_stream, head_azim, tail_azim):
    streams = lax.axis_size("stream")
    azims = lax.axis_size("azim")
    return (
        lax.ppermute(tail_stream, "stream", [(i, i + 1) for i in range(streams - 1)]),
        lax.ppermute(head_stream, "stream", [(i + 1, i) for i in range(streams - 1)]),
        lax.ppermute(tail_azim, "azim", [(i, (i + 1) % azims) for i in range(azims)]),
        lax.ppermute(head_azim, "azim", [((i + 1) % azims, i) for i in range(azims)]),
    )


def on_device(fluid, bubbles, counts, outgoing_block_order, tiles_first_update, tiles_after):
    halos = exchange(fluid[:, 0], fluid[:, -1], fluid[:, :, 0], fluid[:, :, -1])
    rows = fluid.reshape(4, -1, CR)
    packed, places, source = first_bubbles(
        counts, outgoing_block_order, tiles_first_update, bubbles.transpose(1, 0, 2), rows
    )
    packed, halos = lax.optimization_barrier((packed, halos))
    arrived = lax.all_to_all(packed, ("stream", "azim"), split_axis=0, concat_axis=0, tiled=True)
    flow, *faces = first_flow(counts, tiles_first_update, places, source, rows, halos)
    flow, moved, void = second_update(tiles_after, arrived, flow, exchange(*faces))
    return flow.reshape(fluid.shape), moved.transpose(1, 0, 2), void.reshape(fluid.shape[1:])


def solution(mesh):
    return jax.shard_map(
        on_device,
        mesh=mesh,
        in_specs=(
            P(None, "stream", "azim", None),
            P(("stream", "azim"), None, None),
            P(("stream", "azim")),
            P(("stream", "azim")),
            P(("stream", "azim")),
            P(("stream", "azim")),
        ),
        out_specs=(
            P(None, "stream", "azim", None),
            P(("stream", "azim"), None, None),
            P("stream", "azim", None),
        ),
        check_vma=False,
    )
```

```python
import functools

import jax
import jax.numpy as jnp
from jax import lax
from jax.experimental import pallas as pl
from jax.experimental.pallas import tpu as pltpu
from jax.sharding import PartitionSpec as P

SUBSTEPS = 8
TIME_STEP = 0.25
MEAN_FLOW = 0.5
DIFFUSION = 0.1
KERNEL_WIDTH = 1.5
GAS_INDEX = 4.2
PRESSURE_COUPLING = 0.3
AMBIENT = 1.0
RELAX_TIME = 0.5
VISCOUS = 0.08
SOURCE_GAIN = 0.05
VOID_SCALE = 0.01
FOUR_PI = 12.566370614359172
LOG2_E = 1.4426950408889634

CR = 128
BB = 128
NBLK = 512
COMPS = 5
CAP = 4
PACK = 24
GROUP = 8
AZIMS = 32
SLAB = 8
VMEM_MIB = 52
WIDE_MIB = 58
FIRST_BATCH = 64
SECOND_BATCH = 32
CHUNK = 64
SHARP = 0.5 / (KERNEL_WIDTH * KERNEL_WIDTH) * LOG2_E
VMEM = pltpu.VMEM
SMEM = pltpu.SMEM
ANY = pl.BlockSpec(memory_space=pl.ANY)
DIRECT = pl.BlockSpec(memory_space=pltpu.VMEM)


def split(values):
    high = values.astype(jnp.bfloat16)
    low = (values - high.astype(jnp.float32)).astype(jnp.bfloat16)
    return high, low


def centre_terms(position):
    centre = jnp.clip(jnp.floor(position + 0.5), 0.0, CR - 1.0)
    return centre * SHARP, 2.0 * position - centre


def raw_weights(cells, scaled_cells, near, far):
    return jnp.exp2((scaled_cells[...] - near) * (far - cells[...]))


def fill_cells(cells, scaled_cells):
    index = lax.broadcasted_iota(jnp.int32, (CR, BB), 0).astype(jnp.float32)
    cells[...] = index
    scaled_cells[...] = index * SHARP


def sample_phase(size, batches, positions, tile_of, row_of, rows_p, rows_v, cells, scaled_cells, sampled_p, sampled_v):
    sublane = lax.broadcasted_iota(jnp.int32, (GROUP, BB), 0)
    ones = jnp.ones((16, CR), jnp.bfloat16)

    def one(base):
        here = pl.ds(base, GROUP)
        near, far = centre_terms(positions(here))
        rows = jnp.concatenate([rows_p[here, :], rows_v[here, :]], axis=0)
        high, low = split(rows)
        left = jnp.concatenate([high, low, ones], axis=0)
        left = jnp.concatenate([left, left], axis=1)
        acc_p = jnp.zeros((GROUP, BB), jnp.float32)
        acc_v = acc_p
        acc_n = acc_p
        for i in range(0, GROUP, 2):
            right = jnp.concatenate(
                [
                    jnp.concatenate(
                        split(raw_weights(cells, scaled_cells, near[b : b + 1], far[b : b + 1])), axis=0
                    )
                    for b in (i, i + 1)
                ],
                axis=1,
            )
            both = jnp.dot(left, right, preferred_element_type=jnp.float32)
            for b, out in ((i, both[:, :BB]), (i + 1, both[:, BB:])):
                mine = sublane == b
                acc_p = jnp.where(mine, out[0:8] + out[16:24], acc_p)
                acc_v = jnp.where(mine, out[8:16] + out[24:32], acc_v)
                acc_n = jnp.where(mine, out[32:40], acc_n)
        sampled_p[here, :] = acc_p / acc_n
        sampled_v[here, :] = acc_v / acc_n

    def gather(base):
        for i in range(size):
            tile = tile_of(base + i)
            rows_p[pl.ds(base + i, 1), :] = row_of(0, tile)
            rows_v[pl.ds(base + i, 1), :] = row_of(3, tile)

    def body(batch, carry):
        for sub in range(size // GROUP):
            one(pl.multiple_of(batch * size + sub * GROUP, GROUP))
        gather(jnp.minimum(batch + 1, batches - 1) * size)
        return carry

    gather(0)
    lax.fori_loop(0, batches, body, 0)


def bubble_phase(chunks, component, state, sampled_p, sampled_v, places, source, void):
    h = TIME_STEP / SUBSTEPS

    def body(chunk, carry):
        here = pl.ds(pl.multiple_of(chunk * CHUNK, CHUNK), CHUNK)
        radius = component(0, here)
        growth = component(1, here)
        position = component(2, here)
        speed = component(3, here)
        rest_log = jnp.log2(component(4, here))
        drive = AMBIENT + PRESSURE_COUPLING * sampled_p[here, :]
        velocity = sampled_v[here, :]
        for _ in range(SUBSTEPS):
            inverse = 1.0 / radius
            gas = jnp.exp2(GAS_INDEX * (rest_log - jnp.log2(radius)))
            accel = (gas - drive - growth * (1.5 * growth + VISCOUS * inverse)) * inverse
            growth = growth + h * accel
            radius = radius + h * growth
            speed = speed + (h / RELAX_TIME) * (velocity - speed)
            position = position + h * speed
        state[here, 0, :] = radius
        state[here, 1, :] = growth
        state[here, 2, :] = position
        state[here, 3, :] = speed
        state[here, 4, :] = component(4, here)
        places[here, :] = position
        area = radius * radius
        source[here, :] = (SOURCE_GAIN * FOUR_PI) * area * growth
        if void is not None:
            void[here, :] = (VOID_SCALE * FOUR_PI / 3.0) * area * radius
        return carry

    lax.fori_loop(0, chunks, body, 0)


def spread_phase(size, batches, live_blocks, tile_of, places, amounts, cells, scaled_cells, grids, beside):
    sublane = lax.broadcasted_iota(jnp.int32, (GROUP, BB), 0)
    kinds = len(amounts)

    def one(base):
        here = pl.ds(base, GROUP)
        near, far = centre_terms(places[here, :])
        whole = jnp.concatenate([a[here, :] for a in amounts], axis=0)
        accs = [jnp.zeros((GROUP, CR), jnp.float32) for _ in amounts]
        for i in range(0, GROUP, 2):
            lefts = []
            rights = []
            for b in (i, i + 1):
                w = raw_weights(cells, scaled_cells, near[b : b + 1], far[b : b + 1])
                total = jnp.sum(w, axis=0, keepdims=True)
                rights.append(jnp.concatenate(split(w), axis=1))
                left = jnp.concatenate(split(whole * (1.0 / total)), axis=0)
                lefts.append(jnp.concatenate([left, left], axis=1))
            left = jnp.concatenate(lefts, axis=0)
            right = jnp.concatenate(rights, axis=0)
            both = lax.dot_general(
                left, right, (((1,), (1,)), ((), ())), preferred_element_type=jnp.float32
            )
            for b in (0, 1):
                out = both[2 * GROUP * kinds * b :, CR * b : CR * (b + 1)]
                mine = sublane == i + b
                for kind in range(kinds):
                    lo = GROUP * kind
                    hi = GROUP * (kinds + kind)
                    accs[kind] = jnp.where(
                        mine, out[lo : lo + GROUP] + out[hi : hi + GROUP], accs[kind]
                    )
        alive = sublane + base < live_blocks
        accs = [jnp.where(alive, acc, 0.0) for acc in accs]
        return base, accs

    def body(batch, carry):
        done = [one(pl.multiple_of(batch * size + sub * GROUP, GROUP)) for sub in range(size // GROUP)]
        for base, accs in done:
            for i in range(GROUP):
                tile = tile_of(base + i)
                for grid, acc in zip(grids, accs):
                    grid[pl.ds(tile, 1), :] = grid[pl.ds(tile, 1), :] + acc[i : i + 1]
        if beside is not None:
            beside(batch)
        return carry

    lax.fori_loop(0, batches, body, 0)


def first_bubbles_kernel(
    counts, order, tiles, bubbles, flow_p, flow_v, packed, places, source,
    state, rows_p, rows_v, sampled_p, sampled_v, cells, scaled_cells,
):
    size = FIRST_BATCH
    live = counts[0]
    batches = (live + size - 1) // size
    chunks = (live + CHUNK - 1) // CHUNK
    fill_cells(cells, scaled_cells)
    sample_phase(
        size, batches, lambda here: bubbles[2, here, :], lambda j: tiles[j],
        lambda c, tile: (flow_v if c else flow_p)[0, pl.ds(tile, 1), :], rows_p, rows_v,
        cells, scaled_cells, sampled_p, sampled_v,
    )
    bubble_phase(
        chunks, lambda c, here: bubbles[c, here, :], state, sampled_p, sampled_v, places, source, None
    )
    lane = lax.broadcasted_iota(jnp.int32, (PACK - COMPS * CAP, BB), 1)

    def pack(peer, carry):
        flags = jnp.zeros((PACK - COMPS * CAP, BB), jnp.float32)
        for k in range(CAP):
            block = order[peer * CAP + k]
            alive = block < live
            packed[peer, COMPS * k : COMPS * (k + 1), :] = jnp.where(
                alive, state[block, 0:COMPS, :], 0.0
            )
            flags = jnp.where((lane == k) & alive, 1.0, flags)
        packed[peer, COMPS * CAP : PACK, :] = flags
        return carry

    lax.fori_loop(0, NBLK // CAP, pack, 0, unroll=8)


def first_flow_kernel(
    counts, tiles, places, source, flow_in, stream_before, stream_after, azim_before, azim_after,
    new_out, face_0, face_1, face_2, face_3, flow, new, in_sems, out_sems, source_grid, cells, scaled_cells,
):
    copies = flow_copies(flow_in, stream_before, stream_after, flow, in_sems)
    for copy in copies:
        copy.start()
    size = FIRST_BATCH
    live = counts[0]
    fill_cells(cells, scaled_cells)
    source_grid[...] = jnp.zeros_like(source_grid)
    spread_phase(
        size, (live + size - 1) // size, live, lambda j: tiles[j], places, [source], cells, scaled_cells,
        [source_grid], None,
    )
    for copy in copies:
        copy.wait()
    flow_update(flow, source_grid, azim_before, azim_after, new, new_out, out_sems, face_2, face_3)
    streams = new.shape[1] // AZIMS
    face_0[...] = new[:, 0:AZIMS, :]
    face_1[...] = new[:, (streams - 1) * AZIMS :, :]
    flow_stored(new, new_out, out_sems)


def second_kernel(
    tiles, packed, flow_in, stream_before, stream_after, azim_before, azim_after,
    new_out, moved_out, void_out,
    flow, new, in_sems, out_sems, source_grid, void_grid, bubbles_out, moved_sem, void_sem,
    slots, flags, flag_sem, places, source, void,
    state, rows_p, rows_v, sampled_p, sampled_v, cells, scaled_cells,
):
    copies = flow_copies(flow_in, stream_before, stream_after, flow, in_sems)
    for copy in copies:
        copy.start()
    size = SECOND_BATCH
    copy = pltpu.make_async_copy(packed.at[:, COMPS * CAP, :], flags, flag_sem)
    copy.start()
    fill_cells(cells, scaled_cells)
    source_grid[...] = jnp.zeros_like(source_grid)
    void_grid[...] = jnp.zeros_like(void_grid)

    bubbles_out[...] = jnp.zeros_like(bubbles_out)
    copy.wait()

    def unpack(peer, live):
        for k in range(CAP):
            slot = peer * CAP + k
            state[live, 0:COMPS, :] = packed[peer, COMPS * k : COMPS * (k + 1), :]
            slots[live] = slot
            live = live + jnp.where(flags[peer, k] > 0.5, 1, 0)
        return live

    live = lax.fori_loop(0, NBLK // CAP, unpack, jnp.int32(0), unroll=4)
    last = slots[jnp.maximum(live - 1, 0)]
    for i in range(size):
        slots[live + i] = last
        state[jnp.minimum(live + i, NBLK - 1), 0:COMPS, :] = state[jnp.maximum(live - 1, 0), 0:COMPS, :]
    batches = (live + size - 1) // size
    chunks = (live + CHUNK - 1) // CHUNK
    for copy in copies[:2]:
        copy.wait()
    sample_phase(
        size, batches, lambda here: state[here, 2, :], lambda j: tiles[slots[j]],
        lambda c, tile: flow[c, pl.ds(tile + AZIMS, 1), :], rows_p, rows_v,
        cells, scaled_cells, sampled_p, sampled_v,
    )
    bubble_phase(
        chunks, lambda c, here: state[here, c, :], state, sampled_p, sampled_v, places, source, void
    )

    def put(batch):
        for i in range(size):
            j = batch * size + i
            slot = slots[j]
            for c in range(COMPS):
                bubbles_out[c, pl.ds(slot, 1), :] = state[j, c : c + 1, :]

    spread_phase(
        size, batches, live, lambda j: tiles[slots[j]], places, [source, void], cells, scaled_cells,
        [source_grid, void_grid], put,
    )
    moved_copy = pltpu.make_async_copy(bubbles_out, moved_out, moved_sem)
    void_copy = pltpu.make_async_copy(void_grid, void_out, void_sem)
    moved_copy.start()
    void_copy.start()
    for copy in copies[2:]:
        copy.wait()
    flow_update(flow, source_grid, azim_before, azim_after, new, new_out, out_sems)
    moved_copy.wait()
    void_copy.wait()
    flow_stored(new, new_out, out_sems)


def flow_copies(flow_in, stream_before, stream_after, flow, sems):
    tiles = flow_in.shape[1]
    parts = [(flow_in.at[c], flow.at[c, AZIMS : AZIMS + tiles]) for c in (0, 3, 1, 2)]
    parts.append((stream_before, flow.at[:, 0:AZIMS]))
    parts.append((stream_after, flow.at[:, AZIMS + tiles : AZIMS + tiles + AZIMS]))
    return [pltpu.make_async_copy(src, dst, sems.at[i]) for i, (src, dst) in enumerate(parts)]


def slab_copy(slab, new, new_out, sems):
    here = pl.ds(pl.multiple_of(slab * SLAB * AZIMS, SLAB * AZIMS), SLAB * AZIMS)
    return pltpu.make_async_copy(new.at[:, here], new_out.at[:, here], sems.at[slab])


def flow_stored(new, new_out, sems):
    for slab in range(new.shape[1] // AZIMS // SLAB):
        slab_copy(slab, new, new_out, sems).wait()


def flow_update(flow, source, azim_before, azim_after, new, new_out, sems, *faces):
    shape = (AZIMS, CR)
    lane = lax.broadcasted_iota(jnp.int32, shape, 1)
    row = lax.broadcasted_iota(jnp.int32, shape, 0)
    first_lane, last_lane = lane == 0, lane == CR - 1
    first_row, last_row = row == 0, row == AZIMS - 1
    a = 0.5 * TIME_STEP

    def plane(s):
        start = pl.multiple_of(s * AZIMS, AZIMS)
        here = pl.ds(start, AZIMS)
        sums = []
        values = []
        stream_slope = []
        azim_slope = {}
        radial_slope = {}
        for c in range(4):
            before = flow[c, here, :]
            f = flow[c, pl.ds(start + AZIMS, AZIMS), :]
            after = flow[c, pl.ds(start + 2 * AZIMS, AZIMS), :]
            left = jnp.where(first_row, azim_before[c, pl.ds(s, 1), :], pltpu.roll(f, 1, 0))
            right = jnp.where(last_row, azim_after[c, pl.ds(s, 1), :], pltpu.roll(f, AZIMS - 1, 0))
            inner = jnp.where(first_lane, 0.0, pltpu.roll(f, 1, 1))
            outer = jnp.where(last_lane, 0.0, pltpu.roll(f, CR - 1, 1))
            values.append(f)
            sums.append(((before + after) + (left + right)) + (inner + outer))
            stream_slope.append(after - before)
            if c in (0, 2):
                azim_slope[c] = right - left
            if c in (0, 3):
                radial_slope[c] = outer - inner
        rates = [
            MEAN_FLOW * stream_slope[0] + stream_slope[1] + azim_slope[2] + radial_slope[3],
            MEAN_FLOW * stream_slope[1] + stream_slope[0],
            MEAN_FLOW * stream_slope[2] + azim_slope[0],
            MEAN_FLOW * stream_slope[3] + radial_slope[0],
        ]
        for c in range(4):
            value = (1.0 - 6.0 * DIFFUSION) * values[c] + DIFFUSION * sums[c] - a * rates[c]
            if c == 0:
                value = value - TIME_STEP * source[here, :]
            new[c, here, :] = value
            if faces:
                faces[0][c, pl.ds(s, 1), :] = value[0:1]
                faces[1][c, pl.ds(s, 1), :] = value[AZIMS - 1 : AZIMS]

    def body(slab, carry):
        for i in range(SLAB):
            plane(slab * SLAB + i)
        slab_copy(slab, new, new_out, sems).start()
        return carry

    lax.fori_loop(0, new.shape[1] // AZIMS // SLAB, body, 0)


F32 = jnp.float32
SHAPE = jax.ShapeDtypeStruct


def whole(shape):
    return pl.BlockSpec(shape, lambda *_: (0,) * len(shape), memory_space=VMEM)


def component(c, tiles):
    return pl.BlockSpec((1, tiles, CR), lambda *_: (c, 0, 0), memory_space=VMEM)


def params(mib=VMEM_MIB):
    return pltpu.CompilerParams(vmem_limit_bytes=mib << 20)


def bubble_scratch():
    return [VMEM((NBLK, 8, BB), F32)] + [VMEM((NBLK, BB), F32)] * 4 + [VMEM((CR, BB), F32)] * 2


def first_bubbles(counts, order, tiles, bubbles, flow_rows):
    ntile = flow_rows.shape[1]
    peers = NBLK // CAP
    return pl.pallas_call(
        first_bubbles_kernel,
        grid=(1,),
        in_specs=[pl.BlockSpec(memory_space=SMEM)] * 3
        + [whole((COMPS, NBLK, BB)), component(0, ntile), component(3, ntile)],
        out_specs=[whole((peers, PACK, BB))] + [whole((NBLK, BB))] * 2,
        out_shape=[SHAPE((peers, PACK, BB), F32)] + [SHAPE((NBLK, BB), F32)] * 2,
        scratch_shapes=bubble_scratch(),
        compiler_params=params(WIDE_MIB),
        cost_estimate=pl.CostEstimate(flops=10**9, bytes_accessed=10**8, transcendentals=10**7),
        name="first_bubbles",
    )(counts, order, tiles, bubbles, flow_rows, flow_rows)


def faces_kernel(flow, face_0, face_1, face_2, face_3, sems):
    streams, azims = flow.shape[1:3]
    parts = [
        (flow.at[:, :, 0], face_2),
        (flow.at[:, :, azims - 1], face_3),
        (flow.at[:, 0], face_0),
        (flow.at[:, streams - 1], face_1),
    ]
    copies = [pltpu.make_async_copy(src, dst, sems.at[i]) for i, (src, dst) in enumerate(parts)]
    for copy in copies:
        copy.start()
    for copy in copies:
        copy.wait()


def faces_of(flow):
    streams, azims = flow.shape[1:3]
    return pl.pallas_call(
        faces_kernel,
        in_specs=[ANY],
        out_specs=[DIRECT] * 4,
        out_shape=[SHAPE((4, azims, CR), F32)] * 2 + [SHAPE((4, streams, CR), F32)] * 2,
        scratch_shapes=[pltpu.SemaphoreType.DMA((4,))],
        compiler_params=params(WIDE_MIB),
        cost_estimate=pl.CostEstimate(flops=1000, bytes_accessed=10**6, transcendentals=0),
        name="faces",
    )(flow)


def flow_scratch(streams):
    return [
        VMEM((4, (streams + 2) * AZIMS, CR), F32),
        VMEM((4, streams * AZIMS, CR), F32),
        pltpu.SemaphoreType.DMA((6,)),
        pltpu.SemaphoreType.DMA((streams // SLAB,)),
        VMEM((streams * AZIMS, CR), F32),
    ]


def flow_specs():
    return [ANY, DIRECT, DIRECT, DIRECT, DIRECT]


def first_flow(counts, tiles, places, source, flow, halos):
    streams = flow.shape[1] // AZIMS
    return pl.pallas_call(
        first_flow_kernel,
        in_specs=[pl.BlockSpec(memory_space=SMEM)] * 2 + [DIRECT] * 2 + flow_specs(),
        out_specs=[ANY] + [DIRECT] * 4,
        out_shape=[SHAPE(flow.shape, F32)]
        + [SHAPE((4, AZIMS, CR), F32)] * 2
        + [SHAPE((4, streams, CR), F32)] * 2,
        scratch_shapes=flow_scratch(streams) + [VMEM((CR, BB), F32)] * 2,
        compiler_params=params(),
        cost_estimate=pl.CostEstimate(flops=10**9, bytes_accessed=8 * 10**7, transcendentals=10**7),
        name="first_flow",
    )(counts, tiles, places, source, flow, *halos)


def second_update(tiles, packed, flow, halos):
    ntile = flow.shape[1]
    streams = ntile // AZIMS
    peers = NBLK // CAP
    return pl.pallas_call(
        second_kernel,
        in_specs=[pl.BlockSpec(memory_space=SMEM), DIRECT] + flow_specs(),
        out_specs=[ANY] * 3,
        out_shape=[SHAPE(flow.shape, F32), SHAPE((COMPS, NBLK, BB), F32), SHAPE((ntile, CR), F32)],
        scratch_shapes=flow_scratch(streams)
        + [
            VMEM((ntile, CR), F32),
            VMEM((COMPS, NBLK, BB), F32),
            pltpu.SemaphoreType.DMA,
            pltpu.SemaphoreType.DMA,
            SMEM((NBLK + SECOND_BATCH,), jnp.int32),
            SMEM((peers, BB), F32),
            pltpu.SemaphoreType.DMA,
        ]
        + [VMEM((NBLK, BB), F32)] * 3
        + bubble_scratch(),
        compiler_params=params(),
        cost_estimate=pl.CostEstimate(flops=10**9, bytes_accessed=10**8, transcendentals=10**7),
        name="second_update",
    )(tiles, packed, flow, *halos)


def exchange(head_stream, tail_stream, head_azim, tail_azim):
    streams = lax.axis_size("stream")
    azims = lax.axis_size("azim")
    return (
        lax.ppermute(tail_stream, "stream", [(i, i + 1) for i in range(streams - 1)]),
        lax.ppermute(head_stream, "stream", [(i + 1, i) for i in range(streams - 1)]),
        lax.ppermute(tail_azim, "azim", [(i, (i + 1) % azims) for i in range(azims)]),
        lax.ppermute(head_azim, "azim", [((i + 1) % azims, i) for i in range(azims)]),
    )


def on_device(fluid, bubbles, counts, outgoing_block_order, tiles_first_update, tiles_after):
    halos = exchange(*faces_of(fluid))
    rows = fluid.reshape(4, -1, CR)
    packed, places, source = first_bubbles(
        counts, outgoing_block_order, tiles_first_update, bubbles.transpose(1, 0, 2), rows
    )
    packed, halos = lax.optimization_barrier((packed, halos))
    arrived = lax.all_to_all(packed, ("stream", "azim"), split_axis=0, concat_axis=0, tiled=True)
    flow, *faces = first_flow(counts, tiles_first_update, places, source, rows, halos)
    flow, moved, void = second_update(tiles_after, arrived, flow, exchange(*faces))
    return flow.reshape(fluid.shape), moved.transpose(1, 0, 2), void.reshape(fluid.shape[1:])


def solution(mesh):
    return jax.shard_map(
        on_device,
        mesh=mesh,
        in_specs=(
            P(None, "stream", "azim", None),
            P(("stream", "azim"), None, None),
            P(("stream", "azim")),
            P(("stream", "azim")),
            P(("stream", "azim")),
            P(("stream", "azim")),
        ),
        out_specs=(
            P(None, "stream", "azim", None),
            P(("stream", "azim"), None, None),
            P("stream", "azim", None),
        ),
        check_vma=False,
    )
```

```python
import functools

import jax
import jax.numpy as jnp
from jax import lax
from jax.experimental import pallas as pl
from jax.experimental.pallas import tpu as pltpu
from jax.sharding import PartitionSpec as P

SUBSTEPS = 8
TIME_STEP = 0.25
MEAN_FLOW = 0.5
DIFFUSION = 0.1
KERNEL_WIDTH = 1.5
GAS_INDEX = 4.2
PRESSURE_COUPLING = 0.3
AMBIENT = 1.0
RELAX_TIME = 0.5
VISCOUS = 0.08
SOURCE_GAIN = 0.05
VOID_SCALE = 0.01
FOUR_PI = 12.566370614359172
LOG2_E = 1.4426950408889634

CR = 128
BB = 128
NBLK = 512
COMPS = 5
CAP = 4
PACK = 24
GROUP = 8
AZIMS = 32
SLAB = 8
VMEM_MIB = 52
WIDE_MIB = 58
FIRST_BATCH = 64
SPREAD_BATCH = 128
SECOND_BATCH = 32
CHUNK = 64
SHARP = 0.5 / (KERNEL_WIDTH * KERNEL_WIDTH) * LOG2_E
VMEM = pltpu.VMEM
SMEM = pltpu.SMEM
ANY = pl.BlockSpec(memory_space=pl.ANY)
DIRECT = pl.BlockSpec(memory_space=pltpu.VMEM)


def split(values):
    high = values.astype(jnp.bfloat16)
    low = (values - high.astype(jnp.float32)).astype(jnp.bfloat16)
    return high, low


def centre_terms(position):
    centre = jnp.clip(jnp.floor(position + 0.5), 0.0, CR - 1.0)
    return centre * SHARP, 2.0 * position - centre


def raw_weights(cells, scaled_cells, near, far):
    return jnp.exp2((scaled_cells[...] - near) * (far - cells[...]))


def fill_cells(cells, scaled_cells):
    index = lax.broadcasted_iota(jnp.int32, (CR, BB), 0).astype(jnp.float32)
    cells[...] = index
    scaled_cells[...] = index * SHARP


def sample_phase(size, batches, positions, tile_of, row_of, rows_p, rows_v, cells, scaled_cells, sampled_p, sampled_v):
    sublane = lax.broadcasted_iota(jnp.int32, (GROUP, BB), 0)
    ones = jnp.ones((16, CR), jnp.bfloat16)

    def one(base):
        here = pl.ds(base, GROUP)
        near, far = centre_terms(positions(here))
        rows = jnp.concatenate([rows_p[here, :], rows_v[here, :]], axis=0)
        high, low = split(rows)
        left = jnp.concatenate([high, low, ones], axis=0)
        left = jnp.concatenate([left, left], axis=1)
        acc_p = jnp.zeros((GROUP, BB), jnp.float32)
        acc_v = acc_p
        acc_n = acc_p
        for i in range(0, GROUP, 2):
            right = jnp.concatenate(
                [
                    jnp.concatenate(
                        split(raw_weights(cells, scaled_cells, near[b : b + 1], far[b : b + 1])), axis=0
                    )
                    for b in (i, i + 1)
                ],
                axis=1,
            )
            both = jnp.dot(left, right, preferred_element_type=jnp.float32)
            for b, out in ((i, both[:, :BB]), (i + 1, both[:, BB:])):
                mine = sublane == b
                acc_p = jnp.where(mine, out[0:8] + out[16:24], acc_p)
                acc_v = jnp.where(mine, out[8:16] + out[24:32], acc_v)
                acc_n = jnp.where(mine, out[32:40], acc_n)
        sampled_p[here, :] = acc_p / acc_n
        sampled_v[here, :] = acc_v / acc_n

    def gather(base):
        for i in range(size):
            tile = tile_of(base + i)
            rows_p[pl.ds(base + i, 1), :] = row_of(0, tile)
            rows_v[pl.ds(base + i, 1), :] = row_of(3, tile)

    def body(batch, carry):
        for sub in range(size // GROUP):
            one(pl.multiple_of(batch * size + sub * GROUP, GROUP))
        gather(jnp.minimum(batch + 1, batches - 1) * size)
        return carry

    gather(0)
    lax.fori_loop(0, batches, body, 0)


def bubble_phase(chunks, component, state, sampled_p, sampled_v, places, source, void):
    h = TIME_STEP / SUBSTEPS

    def body(chunk, carry):
        here = pl.ds(pl.multiple_of(chunk * CHUNK, CHUNK), CHUNK)
        radius = component(0, here)
        growth = component(1, here)
        position = component(2, here)
        speed = component(3, here)
        rest_log = jnp.log2(component(4, here))
        drive = AMBIENT + PRESSURE_COUPLING * sampled_p[here, :]
        velocity = sampled_v[here, :]
        for _ in range(SUBSTEPS):
            inverse = 1.0 / radius
            gas = jnp.exp2(GAS_INDEX * (rest_log - jnp.log2(radius)))
            accel = (gas - drive - growth * (1.5 * growth + VISCOUS * inverse)) * inverse
            growth = growth + h * accel
            radius = radius + h * growth
            speed = speed + (h / RELAX_TIME) * (velocity - speed)
            position = position + h * speed
        state[here, 0, :] = radius
        state[here, 1, :] = growth
        state[here, 2, :] = position
        state[here, 3, :] = speed
        state[here, 4, :] = component(4, here)
        places[here, :] = position
        area = radius * radius
        source[here, :] = (SOURCE_GAIN * FOUR_PI) * area * growth
        if void is not None:
            void[here, :] = (VOID_SCALE * FOUR_PI / 3.0) * area * radius
        return carry

    lax.fori_loop(0, chunks, body, 0)


def spread_phase(size, batches, live_blocks, tile_of, places, amounts, cells, scaled_cells, grids, beside):
    sublane = lax.broadcasted_iota(jnp.int32, (GROUP, BB), 0)
    kinds = len(amounts)

    def one(base):
        here = pl.ds(base, GROUP)
        near, far = centre_terms(places[here, :])
        whole = jnp.concatenate([a[here, :] for a in amounts], axis=0)
        accs = [jnp.zeros((GROUP, CR), jnp.float32) for _ in amounts]
        for i in range(0, GROUP, 2):
            lefts = []
            rights = []
            for b in (i, i + 1):
                w = raw_weights(cells, scaled_cells, near[b : b + 1], far[b : b + 1])
                total = jnp.sum(w, axis=0, keepdims=True)
                rights.append(jnp.concatenate(split(w), axis=1))
                left = jnp.concatenate(split(whole * (1.0 / total)), axis=0)
                lefts.append(jnp.concatenate([left, left], axis=1))
            left = jnp.concatenate(lefts, axis=0)
            right = jnp.concatenate(rights, axis=0)
            both = lax.dot_general(
                left, right, (((1,), (1,)), ((), ())), preferred_element_type=jnp.float32
            )
            for b in (0, 1):
                out = both[2 * GROUP * kinds * b :, CR * b : CR * (b + 1)]
                mine = sublane == i + b
                for kind in range(kinds):
                    lo = GROUP * kind
                    hi = GROUP * (kinds + kind)
                    accs[kind] = jnp.where(
                        mine, out[lo : lo + GROUP] + out[hi : hi + GROUP], accs[kind]
                    )
        alive = sublane + base < live_blocks
        accs = [jnp.where(alive, acc, 0.0) for acc in accs]
        return base, accs

    def body(batch, carry):
        done = [one(pl.multiple_of(batch * size + sub * GROUP, GROUP)) for sub in range(size // GROUP)]
        for base, accs in done:
            for i in range(GROUP):
                tile = tile_of(base + i)
                for grid, acc in zip(grids, accs):
                    grid[pl.ds(tile, 1), :] = grid[pl.ds(tile, 1), :] + acc[i : i + 1]
        if beside is not None:
            beside(batch)
        return carry

    lax.fori_loop(0, batches, body, 0)


def first_bubbles_kernel(
    counts, order, tiles, bubbles, flow_p, flow_v, packed, places, source,
    state, rows_p, rows_v, sampled_p, sampled_v, cells, scaled_cells,
):
    size = FIRST_BATCH
    live = counts[0]
    batches = (live + size - 1) // size
    chunks = (live + CHUNK - 1) // CHUNK
    fill_cells(cells, scaled_cells)
    sample_phase(
        size, batches, lambda here: bubbles[2, here, :], lambda j: tiles[j],
        lambda c, tile: (flow_v if c else flow_p)[0, pl.ds(tile, 1), :], rows_p, rows_v,
        cells, scaled_cells, sampled_p, sampled_v,
    )
    bubble_phase(
        chunks, lambda c, here: bubbles[c, here, :], state, sampled_p, sampled_v, places, source, None
    )
    lane = lax.broadcasted_iota(jnp.int32, (PACK - COMPS * CAP, BB), 1)

    def pack(peer, carry):
        flags = jnp.zeros((PACK - COMPS * CAP, BB), jnp.float32)
        for k in range(CAP):
            block = order[peer * CAP + k]
            alive = block < live
            packed[peer, COMPS * k : COMPS * (k + 1), :] = jnp.where(
                alive, state[block, 0:COMPS, :], 0.0
            )
            flags = jnp.where((lane == k) & alive, 1.0, flags)
        packed[peer, COMPS * CAP : PACK, :] = flags
        return carry

    lax.fori_loop(0, NBLK // CAP, pack, 0, unroll=8)


def first_flow_kernel(
    counts, tiles, places, source, flow_in, stream_before, stream_after, azim_before, azim_after,
    new_out, face_0, face_1, face_2, face_3, flow, new, in_sems, out_sems, source_grid, cells, scaled_cells,
):
    copies = flow_copies(flow_in, stream_before, stream_after, flow, in_sems)
    for copy in copies:
        copy.start()
    size = SPREAD_BATCH
    live = counts[0]
    fill_cells(cells, scaled_cells)
    source_grid[...] = jnp.zeros_like(source_grid)
    spread_phase(
        size, (live + size - 1) // size, live, lambda j: tiles[j], places, [source], cells, scaled_cells,
        [source_grid], None,
    )
    for copy in copies:
        copy.wait()
    flow_update(flow, source_grid, azim_before, azim_after, new, new_out, out_sems, face_2, face_3)
    streams = new.shape[1] // AZIMS
    face_0[...] = new[:, 0:AZIMS, :]
    face_1[...] = new[:, (streams - 1) * AZIMS :, :]
    flow_stored(new, new_out, out_sems)


def second_kernel(
    tiles, packed, flow_in, stream_before, stream_after, azim_before, azim_after,
    new_out, moved_out, void_out,
    flow, new, in_sems, out_sems, source_grid, void_grid, bubbles_out, moved_sem, void_sem,
    slots, flags, flag_sem, places, source, void,
    state, rows_p, rows_v, sampled_p, sampled_v, cells, scaled_cells,
):
    copies = flow_copies(flow_in, stream_before, stream_after, flow, in_sems)
    for copy in copies:
        copy.start()
    size = SECOND_BATCH
    copy = pltpu.make_async_copy(packed.at[:, COMPS * CAP, :], flags, flag_sem)
    copy.start()
    fill_cells(cells, scaled_cells)
    source_grid[...] = jnp.zeros_like(source_grid)
    void_grid[...] = jnp.zeros_like(void_grid)

    bubbles_out[...] = jnp.zeros_like(bubbles_out)
    copy.wait()

    def unpack(peer, live):
        for k in range(CAP):
            slot = peer * CAP + k
            state[live, 0:COMPS, :] = packed[peer, COMPS * k : COMPS * (k + 1), :]
            slots[live] = slot
            live = live + jnp.where(flags[peer, k] > 0.5, 1, 0)
        return live

    live = lax.fori_loop(0, NBLK // CAP, unpack, jnp.int32(0), unroll=4)
    last = slots[jnp.maximum(live - 1, 0)]
    for i in range(size):
        slots[live + i] = last
        state[jnp.minimum(live + i, NBLK - 1), 0:COMPS, :] = state[jnp.maximum(live - 1, 0), 0:COMPS, :]
    batches = (live + size - 1) // size
    chunks = (live + CHUNK - 1) // CHUNK
    for copy in copies[:2]:
        copy.wait()
    sample_phase(
        size, batches, lambda here: state[here, 2, :], lambda j: tiles[slots[j]],
        lambda c, tile: flow[c, pl.ds(tile + AZIMS, 1), :], rows_p, rows_v,
        cells, scaled_cells, sampled_p, sampled_v,
    )
    bubble_phase(
        chunks, lambda c, here: state[here, c, :], state, sampled_p, sampled_v, places, source, void
    )

    def put(batch):
        for i in range(size):
            j = batch * size + i
            slot = slots[j]
            for c in range(COMPS):
                bubbles_out[c, pl.ds(slot, 1), :] = state[j, c : c + 1, :]

    spread_phase(
        size, batches, live, lambda j: tiles[slots[j]], places, [source, void], cells, scaled_cells,
        [source_grid, void_grid], put,
    )
    moved_copy = pltpu.make_async_copy(bubbles_out, moved_out, moved_sem)
    void_copy = pltpu.make_async_copy(void_grid, void_out, void_sem)
    moved_copy.start()
    void_copy.start()
    for copy in copies[2:]:
        copy.wait()
    flow_update(flow, source_grid, azim_before, azim_after, new, new_out, out_sems)
    moved_copy.wait()
    void_copy.wait()
    flow_stored(new, new_out, out_sems)


def flow_copies(flow_in, stream_before, stream_after, flow, sems):
    tiles = flow_in.shape[1]
    parts = [(flow_in.at[c], flow.at[c, AZIMS : AZIMS + tiles]) for c in (0, 3, 1, 2)]
    parts.append((stream_before, flow.at[:, 0:AZIMS]))
    parts.append((stream_after, flow.at[:, AZIMS + tiles : AZIMS + tiles + AZIMS]))
    return [pltpu.make_async_copy(src, dst, sems.at[i]) for i, (src, dst) in enumerate(parts)]


def slab_copy(slab, new, new_out, sems):
    here = pl.ds(pl.multiple_of(slab * SLAB * AZIMS, SLAB * AZIMS), SLAB * AZIMS)
    return pltpu.make_async_copy(new.at[:, here], new_out.at[:, here], sems.at[slab])


def flow_stored(new, new_out, sems):
    for slab in range(new.shape[1] // AZIMS // SLAB):
        slab_copy(slab, new, new_out, sems).wait()


def flow_update(flow, source, azim_before, azim_after, new, new_out, sems, *faces):
    shape = (AZIMS, CR)
    lane = lax.broadcasted_iota(jnp.int32, shape, 1)
    row = lax.broadcasted_iota(jnp.int32, shape, 0)
    first_lane, last_lane = lane == 0, lane == CR - 1
    first_row, last_row = row == 0, row == AZIMS - 1
    a = 0.5 * TIME_STEP

    def plane(s):
        start = pl.multiple_of(s * AZIMS, AZIMS)
        here = pl.ds(start, AZIMS)
        sums = []
        values = []
        stream_slope = []
        azim_slope = {}
        radial_slope = {}
        for c in range(4):
            before = flow[c, here, :]
            f = flow[c, pl.ds(start + AZIMS, AZIMS), :]
            after = flow[c, pl.ds(start + 2 * AZIMS, AZIMS), :]
            left = jnp.where(first_row, azim_before[c, pl.ds(s, 1), :], pltpu.roll(f, 1, 0))
            right = jnp.where(last_row, azim_after[c, pl.ds(s, 1), :], pltpu.roll(f, AZIMS - 1, 0))
            inner = jnp.where(first_lane, 0.0, pltpu.roll(f, 1, 1))
            outer = jnp.where(last_lane, 0.0, pltpu.roll(f, CR - 1, 1))
            values.append(f)
            sums.append(((before + after) + (left + right)) + (inner + outer))
            stream_slope.append(after - before)
            if c in (0, 2):
                azim_slope[c] = right - left
            if c in (0, 3):
                radial_slope[c] = outer - inner
        rates = [
            MEAN_FLOW * stream_slope[0] + stream_slope[1] + azim_slope[2] + radial_slope[3],
            MEAN_FLOW * stream_slope[1] + stream_slope[0],
            MEAN_FLOW * stream_slope[2] + azim_slope[0],
            MEAN_FLOW * stream_slope[3] + radial_slope[0],
        ]
        for c in range(4):
            value = (1.0 - 6.0 * DIFFUSION) * values[c] + DIFFUSION * sums[c] - a * rates[c]
            if c == 0:
                value = value - TIME_STEP * source[here, :]
            new[c, here, :] = value
            if faces:
                faces[0][c, pl.ds(s, 1), :] = value[0:1]
                faces[1][c, pl.ds(s, 1), :] = value[AZIMS - 1 : AZIMS]

    def body(slab, carry):
        for i in range(SLAB):
            plane(slab * SLAB + i)
        slab_copy(slab, new, new_out, sems).start()
        return carry

    lax.fori_loop(0, new.shape[1] // AZIMS // SLAB, body, 0)


F32 = jnp.float32
SHAPE = jax.ShapeDtypeStruct


def whole(shape):
    return pl.BlockSpec(shape, lambda *_: (0,) * len(shape), memory_space=VMEM)


def component(c, tiles):
    return pl.BlockSpec((1, tiles, CR), lambda *_: (c, 0, 0), memory_space=VMEM)


def params(mib=VMEM_MIB):
    return pltpu.CompilerParams(vmem_limit_bytes=mib << 20)


def bubble_scratch():
    return [VMEM((NBLK, 8, BB), F32)] + [VMEM((NBLK, BB), F32)] * 4 + [VMEM((CR, BB), F32)] * 2


def first_bubbles(counts, order, tiles, bubbles, flow_rows):
    ntile = flow_rows.shape[1]
    peers = NBLK // CAP
    return pl.pallas_call(
        first_bubbles_kernel,
        grid=(1,),
        in_specs=[pl.BlockSpec(memory_space=SMEM)] * 3
        + [whole((COMPS, NBLK, BB)), component(0, ntile), component(3, ntile)],
        out_specs=[whole((peers, PACK, BB))] + [whole((NBLK, BB))] * 2,
        out_shape=[SHAPE((peers, PACK, BB), F32)] + [SHAPE((NBLK, BB), F32)] * 2,
        scratch_shapes=bubble_scratch(),
        compiler_params=params(WIDE_MIB),
        cost_estimate=pl.CostEstimate(flops=10**9, bytes_accessed=10**8, transcendentals=10**7),
        name="first_bubbles",
    )(counts, order, tiles, bubbles, flow_rows, flow_rows)


def faces_kernel(flow, face_0, face_1, face_2, face_3, sems):
    streams, azims = flow.shape[1:3]
    parts = [
        (flow.at[:, :, 0], face_2),
        (flow.at[:, :, azims - 1], face_3),
        (flow.at[:, 0], face_0),
        (flow.at[:, streams - 1], face_1),
    ]
    copies = [pltpu.make_async_copy(src, dst, sems.at[i]) for i, (src, dst) in enumerate(parts)]
    for copy in copies:
        copy.start()
    for copy in copies:
        copy.wait()


def faces_of(flow):
    streams, azims = flow.shape[1:3]
    return pl.pallas_call(
        faces_kernel,
        in_specs=[ANY],
        out_specs=[DIRECT] * 4,
        out_shape=[SHAPE((4, azims, CR), F32)] * 2 + [SHAPE((4, streams, CR), F32)] * 2,
        scratch_shapes=[pltpu.SemaphoreType.DMA((4,))],
        compiler_params=params(WIDE_MIB),
        cost_estimate=pl.CostEstimate(flops=1000, bytes_accessed=10**6, transcendentals=0),
        name="faces",
    )(flow)


def flow_scratch(streams):
    return [
        VMEM((4, (streams + 2) * AZIMS, CR), F32),
        VMEM((4, streams * AZIMS, CR), F32),
        pltpu.SemaphoreType.DMA((6,)),
        pltpu.SemaphoreType.DMA((streams // SLAB,)),
        VMEM((streams * AZIMS, CR), F32),
    ]


def flow_specs():
    return [ANY, DIRECT, DIRECT, DIRECT, DIRECT]


def first_flow(counts, tiles, places, source, flow, halos):
    streams = flow.shape[1] // AZIMS
    return pl.pallas_call(
        first_flow_kernel,
        in_specs=[pl.BlockSpec(memory_space=SMEM)] * 2 + [DIRECT] * 2 + flow_specs(),
        out_specs=[ANY] + [DIRECT] * 4,
        out_shape=[SHAPE(flow.shape, F32)]
        + [SHAPE((4, AZIMS, CR), F32)] * 2
        + [SHAPE((4, streams, CR), F32)] * 2,
        scratch_shapes=flow_scratch(streams) + [VMEM((CR, BB), F32)] * 2,
        compiler_params=params(),
        cost_estimate=pl.CostEstimate(flops=10**9, bytes_accessed=8 * 10**7, transcendentals=10**7),
        name="first_flow",
    )(counts, tiles, places, source, flow, *halos)


def second_update(tiles, packed, flow, halos):
    ntile = flow.shape[1]
    streams = ntile // AZIMS
    peers = NBLK // CAP
    return pl.pallas_call(
        second_kernel,
        in_specs=[pl.BlockSpec(memory_space=SMEM), DIRECT] + flow_specs(),
        out_specs=[ANY] * 3,
        out_shape=[SHAPE(flow.shape, F32), SHAPE((COMPS, NBLK, BB), F32), SHAPE((ntile, CR), F32)],
        scratch_shapes=flow_scratch(streams)
        + [
            VMEM((ntile, CR), F32),
            VMEM((COMPS, NBLK, BB), F32),
            pltpu.SemaphoreType.DMA,
            pltpu.SemaphoreType.DMA,
            SMEM((NBLK + SECOND_BATCH,), jnp.int32),
            SMEM((peers, BB), F32),
            pltpu.SemaphoreType.DMA,
        ]
        + [VMEM((NBLK, BB), F32)] * 3
        + bubble_scratch(),
        compiler_params=params(),
        cost_estimate=pl.CostEstimate(flops=10**9, bytes_accessed=10**8, transcendentals=10**7),
        name="second_update",
    )(tiles, packed, flow, *halos)


def exchange(head_stream, tail_stream, head_azim, tail_azim):
    streams = lax.axis_size("stream")
    azims = lax.axis_size("azim")
    return (
        lax.ppermute(tail_stream, "stream", [(i, i + 1) for i in range(streams - 1)]),
        lax.ppermute(head_stream, "stream", [(i + 1, i) for i in range(streams - 1)]),
        lax.ppermute(tail_azim, "azim", [(i, (i + 1) % azims) for i in range(azims)]),
        lax.ppermute(head_azim, "azim", [((i + 1) % azims, i) for i in range(azims)]),
    )


def on_device(fluid, bubbles, counts, outgoing_block_order, tiles_first_update, tiles_after):
    halos = exchange(*faces_of(fluid))
    rows = fluid.reshape(4, -1, CR)
    packed, places, source = first_bubbles(
        counts, outgoing_block_order, tiles_first_update, bubbles.transpose(1, 0, 2), rows
    )
    packed, halos = lax.optimization_barrier((packed, halos))
    arrived = lax.all_to_all(packed, ("stream", "azim"), split_axis=0, concat_axis=0, tiled=True)
    flow, *faces = first_flow(counts, tiles_first_update, places, source, rows, halos)
    flow, moved, void = second_update(tiles_after, arrived, flow, exchange(*faces))
    return flow.reshape(fluid.shape), moved.transpose(1, 0, 2), void.reshape(fluid.shape[1:])


def solution(mesh):
    return jax.shard_map(
        on_device,
        mesh=mesh,
        in_specs=(
            P(None, "stream", "azim", None),
            P(("stream", "azim"), None, None),
            P(("stream", "azim")),
            P(("stream", "azim")),
            P(("stream", "azim")),
            P(("stream", "azim")),
        ),
        out_specs=(
            P(None, "stream", "azim", None),
            P(("stream", "azim"), None, None),
            P("stream", "azim", None),
        ),
        check_vma=False,
    )
```
